256 devices in a mesh: dp: 32 (over y_hi, z, core), pipe: 2 (over y_lo), mp: 4 (over x).
Axes of the slice: x: 4, y: 4 (y_hi: 2, y_lo: 2; y = y_hi * 2 + y_lo), z: 8, core: 2. Of those that a mesh axis runs over, the one named last changes fastest.
Arguments:
- streams: bfloat16 [2, 64, 128, 2048], P('pipe', 'dp', None, 'mp'), may hold values from -14 to 14
- lengths: int32 [64], P('dp'), may hold values from 32 to 128, as said below
- encoder_gain: bfloat16 [2048], replicated, may hold values from 0.25 to 1.75
- ffn_gate: bfloat16 [2048, 8192], P('dp', 'mp'), may hold values from -0.125 to 0.125
- ffn_lift: bfloat16 [2048, 8192], P('dp', 'mp'), may hold values from -0.125 to 0.125
- ffn_down: bfloat16 [8192, 2048], P('mp', 'dp'), may hold values from -0.0625 to 0.0625
- final_gain: bfloat16 [2048], P('mp'), may hold values from 0.25 to 1.75
- decoder_gain: bfloat16 [2048], replicated, may hold values from 0.25 to 1.75
- query_weight: bfloat16 [2048, 2048], P(None, 'mp'), may hold values from -0.15191747 to 0.15191747
- key_weight: bfloat16 [2048, 2048], P(None, 'mp'), may hold values from -0.125 to 0.125
- value_weight: bfloat16 [2048, 2048], P(None, 'mp'), may hold values from -0.125 to 0.125
- output_weight: bfloat16 [2048, 2048], P('mp'), may hold values from -0.125 to 0.125
Outputs:
- sections: bfloat16 [2, 64, 128, 2048], P('pipe', 'dp', None, 'mp')
The draws below stay inside these ranges and needn't reach their ends.
Inputs may be any that keep to these rules, and one draw needn't show every extreme that they name: `lengths`: every draw holds an example with 128 unpadded tokens and one with a quarter of 128.
All inputs are finite; a program needn't handle non-finite values.
Results may differ from the reference program's by a relative error of at most 0.024.
The reference program's roundings to bfloat16 on the way (of `normed`, `hidden`, `memory`, `query_in`, `probs` and `context`) count: a program that leaves them out, or rounds other values in their place, can miss the bound.
Values may be sent and summed in bfloat16 or wider, within the bound.
No kernel may reach another device: no remote copies, remote signals or barrier semaphores. Data moves between devices by JAX's collectives and lax.ppermute only.
A program may use at most 128 MiB of HBM per device.

```python
import math
import jax
import jax.numpy as jnp
from jax import lax

D = 2048
FF = 8192
HEADS = 8
HEAD_DIM = 256
LEN = 128
EXAMPLES = 64


def draw_streams(key, part):
    key = jax.random.fold_in(key, 11)
    first, second, third = jax.random.split(key, 3)
    base = jax.random.truncated_normal(first, -4.0, 4.0, (2, EXAMPLES, LEN, D), jnp.float32)
    rise = math.log(3.0)
    row_scale = jnp.exp(jax.random.uniform(second, (2, EXAMPLES, LEN, 1), jnp.float32, math.log(0.1), 0.0))
    position = jnp.arange(D, dtype=jnp.float32) / D
    column_scale = jnp.exp(rise * (position - 1.0) + jax.random.uniform(third, (2, 1, 1, D), jnp.float32, -1.2, 1.2))
    return (base * row_scale * column_scale).astype(jnp.bfloat16)


def draw_lengths(key, part):
    key = jax.random.fold_in(key, 23)
    first, second = jax.random.split(key)
    counts = jax.random.randint(first, (EXAMPLES,), LEN // 4, LEN + 1)
    spots = jax.random.permutation(second, EXAMPLES)
    position = jnp.arange(EXAMPLES)
    counts = jnp.where(position == spots[0], LEN, counts)
    counts = jnp.where(position == spots[1], LEN // 4, counts)
    return counts.astype(jnp.int32)


def draw_query_weight(key, part):
    key = jax.random.fold_in(key, 37)
    base = jax.random.truncated_normal(key, -3.0, 3.0, (D, HEADS * HEAD_DIM), jnp.float32)
    return (base / math.sqrt(D * HEAD_DIM)).astype(jnp.bfloat16)


def block_scale(own_key, dims, cuts, smallest, largest):
    level, own = 1.0, jax.random.fold_in(own_key, 6)
    for axis_at, blocks in cuts:
        draws = jnp.exp(jax.random.uniform(jax.random.fold_in(own, axis_at), (blocks,), jnp.float32, smallest / len(cuts), largest / len(cuts)))
        level = level * jnp.repeat(draws, dims[axis_at] // blocks).reshape([-1 if axis == axis_at else 1 for axis in range(len(dims))])
    return level


def normal_values(own_key, extent, spread, most, shards=(), kind=jnp.bfloat16):
    factor_of = block_scale(own_key, extent, shards, -0.22, 0.18) if shards else 1.0
    array = jax.random.normal(own_key, extent, jnp.float32) * spread * factor_of
    return jnp.minimum(jnp.maximum(array, -most), most).astype(kind)


def setup_inputs(seed: int = 0) -> dict:
    seeds = jax.random.split(jax.random.key(seed), 13)
    return {
        "streams": draw_streams(jax.random.fold_in(seeds[12], 71), 0),
        "lengths": draw_lengths(jax.random.fold_in(seeds[12], 71), 0),
        "encoder_gain": jnp.clip(1.0 + 0.15 * jax.random.normal(seeds[2], (D,), jnp.float32), 0.25, 1.75).astype(jnp.bfloat16),
        "ffn_gate": normal_values(seeds[3], (D, FF), D ** -0.5, 0.125, ((0, 32), (1, 4))),
        "ffn_lift": normal_values(seeds[4], (D, FF), D ** -0.5, 0.125, ((0, 32), (1, 4))),
        "ffn_down": normal_values(seeds[5], (FF, D), FF ** -0.5, 0.0625, ((0, 4), (1, 32))),
        "final_gain": jnp.clip(1.0 + 0.15 * jax.random.normal(seeds[6], (D,), jnp.float32), 0.25, 1.75).astype(jnp.bfloat16),
        "decoder_gain": jnp.clip(1.0 + 0.15 * jax.random.normal(seeds[7], (D,), jnp.float32), 0.25, 1.75).astype(jnp.bfloat16),
        "query_weight": draw_query_weight(jax.random.fold_in(seeds[12], 71), 0),
        "key_weight": normal_values(seeds[9], (D, HEADS * HEAD_DIM), D ** -0.5, 0.125, ((1, 4),)),
        "value_weight": normal_values(seeds[10], (D, HEADS * HEAD_DIM), D ** -0.5, 0.125, ((1, 4),)),
        "output_weight": normal_values(seeds[11], (HEADS * HEAD_DIM, D), (HEADS * HEAD_DIM) ** -0.5, 0.125, ((0, 4),)),
    }


epsilon = 1e-06

def scale_rows(values, gain):
    mean_square = lax.optimization_barrier(jnp.mean(values * values, axis=-1, keepdims=True))
    return values * lax.rsqrt(mean_square + epsilon) * gain.astype(jnp.float32)

def reference(streams, lengths, encoder_gain, ffn_gate, ffn_lift, ffn_down, final_gain, decoder_gain, query_weight, key_weight, value_weight, output_weight):
    total = EXAMPLES * LEN
    encoded = streams[0].reshape(total, D).astype(jnp.float32)
    decoding = streams[1].reshape(total, D).astype(jnp.float32)
    normed = scale_rows(encoded, encoder_gain).astype(jnp.bfloat16)
    gate = jnp.dot(normed, ffn_gate, preferred_element_type=jnp.float32)
    lift = jnp.dot(normed, ffn_lift, preferred_element_type=jnp.float32)
    hidden = (jax.nn.gelu(gate, approximate=True) * lift).astype(jnp.bfloat16)
    ffn = jnp.dot(hidden, ffn_down, preferred_element_type=jnp.float32)
    memory = scale_rows(encoded + ffn, final_gain).astype(jnp.bfloat16)
    query_in = scale_rows(decoding, decoder_gain).astype(jnp.bfloat16)
    shape4 = (EXAMPLES, LEN, HEADS, HEAD_DIM)
    queries = jnp.dot(query_in, query_weight, preferred_element_type=jnp.float32).astype(jnp.bfloat16).reshape(shape4)
    keys = jnp.dot(memory, key_weight, preferred_element_type=jnp.float32).astype(jnp.bfloat16).reshape(shape4)
    values = jnp.dot(memory, value_weight, preferred_element_type=jnp.float32).astype(jnp.bfloat16).reshape(shape4)
    scores = jnp.einsum('eqhd,ekhd->ehqk', queries.astype(jnp.float32), keys.astype(jnp.float32))
    positions = jnp.arange(LEN, dtype=jnp.int32)
    valid = (positions[None, :] < lengths.astype(jnp.int32)[:, None])[:, None, None, :]
    scores = jnp.where(valid, scores, -1e+30)
    highest = lax.optimization_barrier(jnp.max(scores, axis=-1, keepdims=True))
    weights = jnp.exp(scores - highest)
    probs = (weights / lax.optimization_barrier(jnp.sum(weights, axis=-1, keepdims=True))).astype(jnp.bfloat16)
    context = jnp.einsum('ehqk,ekhd->eqhd', probs.astype(jnp.float32), values.astype(jnp.float32))
    context = context.astype(jnp.bfloat16).reshape(total, HEADS * HEAD_DIM)
    attended = jnp.dot(context, output_weight, preferred_element_type=jnp.float32)
    decoded = (decoding + attended).astype(jnp.bfloat16)
    return jnp.stack([memory, decoded]).reshape(2, EXAMPLES, LEN, D)
```

```python
import jax
import jax.numpy as jnp
import numpy as np
from jax import lax
from jax.experimental import pallas as pl
from jax.experimental.pallas import tpu as pltpu
from jax.sharding import Mesh, PartitionSpec as P

HEAD_DIM = 256
epsilon = 1e-06
SIZES = {"yh": 2, "z": 8, "c": 2, "p": 2, "x": 4}
LINE = ("z", "c")
PLANE = ("yh", "p", "x")
bf16, f32 = jnp.bfloat16, jnp.float32
MIB = 1 << 20


def moved(value, axes, route):
    dims = [SIZES[a] for a in axes]
    pairs = []
    for at in np.ndindex(*dims):
        to = route(*at)
        if to is not None:
            pairs.append((int(np.ravel_multi_index(at, dims)), int(np.ravel_multi_index(to, dims))))
    return lax.ppermute(value, axes, pairs)


def gathered(value, axis):
    spread = jnp.broadcast_to(value[None], (SIZES[axis],) + value.shape)
    return lax.all_to_all(spread, axis, 0, 0)


def whole(shape):
    return pl.BlockSpec(shape, lambda *_: (0,) * len(shape))


def ffn_kernel(tokens, gain, weights, out):
    square = 0.0
    for b in range(4):
        t = tokens[b].astype(f32)
        square = square + jnp.sum(t * t, axis=-1, keepdims=True)
    scale = lax.rsqrt(square * (1.0 / 2048) + epsilon)
    gate = lift = 0.0
    for yh in range(2):
        for zz in range(4):
            b, at = yh * 2 + zz // 2, (zz % 2) * 256
            t = tokens[b, :, at : at + 256].astype(f32)
            n = (t * scale * gain[b : b + 1, at : at + 256].astype(f32)).astype(bf16)
            parts = [[weights[zz * 4 + k, yh, m] for k in range(4)] for m in range(2)]
            gate += jnp.dot(n, jnp.concatenate(parts[0], 0), preferred_element_type=f32)
            lift += jnp.dot(n, jnp.concatenate(parts[1], 0), preferred_element_type=f32)
    inner = 0.7978845608028654 * (gate + 0.044715 * (gate * gate * gate))
    hidden = (0.5 * gate * (1.0 + jnp.tanh(inner)) * lift).astype(bf16)
    for yh in range(2):
        for zz in range(4):
            at = yh * 1024 + zz * 256
            down = jnp.concatenate([weights[zz * 4 + k, yh, 2] for k in range(4)], 0)
            part = lax.dot_general(hidden, down, (((1,), (1,)), ((), ())), preferred_element_type=f32)
            out[:, at : at + 256] = part.astype(bf16)


def ffn(tokens, gain, weights):
    rows = tokens.shape[1]
    tile = 256
    return pl.pallas_call(
        ffn_kernel,
        grid=(rows // tile,),
        in_specs=[
            pl.BlockSpec((4, tile, 512), lambda i: (0, i, 0)),
            whole(gain.shape),
            whole(weights.shape),
        ],
        out_specs=pl.BlockSpec((tile, 2048), lambda i: (i, 0)),
        out_shape=jax.ShapeDtypeStruct((rows, 2048), bf16),
        compiler_params=pltpu.CompilerParams(vmem_limit_bytes=48 * MIB),
        cost_estimate=pl.CostEstimate(
            flops=rows * 2048 * 512 * 6, bytes_accessed=10 * MIB, transcendentals=rows * 512
        ),
    )(tokens, gain, weights)


def memory_kernel(terms, tokens, gain, out):
    square, kept = 0.0, []
    for b in range(4):
        at = slice(b * 512, (b + 1) * 512)
        total = terms[0, :, at].astype(f32)
        for k in range(1, 16):
            total = total + terms[k, :, at].astype(f32)
        merged = tokens[b].astype(f32) + total
        square = square + jnp.sum(merged * merged, axis=-1, keepdims=True)
        kept.append(merged)
    scale = lax.rsqrt(square * (1.0 / 2048) + epsilon)
    for b in range(4):
        at = slice(b * 512, (b + 1) * 512)
        rounded = (kept[b] * scale * gain[b : b + 1].astype(f32)).astype(bf16)
        for k in range(4):
            out[k, :, at] = rounded


def attention_kernel(lengths, query, memory, key_weight, value_weight, output_weight, out):
    source = memory[...]
    keys = jnp.dot(source, key_weight[...], preferred_element_type=f32).astype(bf16)
    values = jnp.dot(source, value_weight[...], preferred_element_type=f32).astype(bf16)
    positions = lax.broadcasted_iota(jnp.int32, (128, 128), 1)
    valid = positions < lengths[0]
    contexts = []
    for h in range(2):
        at = slice(h * HEAD_DIM, (h + 1) * HEAD_DIM)
        scores = lax.dot_general(
            query[:, at], keys[:, at], (((1,), (1,)), ((), ())), preferred_element_type=f32
        )
        scores = jnp.where(valid, scores, -1e30)
        weights = jnp.exp(scores - jnp.max(scores, axis=-1, keepdims=True))
        probs = (weights / jnp.sum(weights, axis=-1, keepdims=True)).astype(bf16)
        contexts.append(jnp.dot(probs, values[:, at], preferred_element_type=f32).astype(bf16))
    context = jnp.concatenate(contexts, axis=1)
    for b in range(4):
        part = jnp.dot(
            context, output_weight[:, b * 512 : (b + 1) * 512], preferred_element_type=f32
        )
        out[b] = part.astype(bf16)


def vmem():
    return pl.BlockSpec(memory_space=pltpu.VMEM)


def shards(
    streams,
    lengths,
    encoder_gain,
    ffn_gate,
    ffn_lift,
    ffn_down,
    final_gain,
    decoder_gain,
    query_weight,
    key_weight,
    value_weight,
    output_weight,
):
    yh, p, x = lax.axis_index("yh"), lax.axis_index("p"), lax.axis_index("x")
    local = streams[0].reshape(256, 512)

    stack = jnp.stack([ffn_gate, ffn_lift, ffn_down.T])

    def quarter(at):
        return lax.dynamic_slice_in_dim(stack, (p * 2 + at) * 512, 512, 2)

    own = quarter(yh)
    other = moved(quarter(1 - yh), ("yh",), lambda a: (1 - a,))
    both = jnp.where(yh == 0, jnp.stack([own, other]), jnp.stack([other, own]))
    weights = lax.all_gather(both, LINE, axis=0)

    swapped = moved(local, ("p",), lambda a: (1 - a,))
    across = moved(local, ("yh", "p"), lambda a, b: (1 - a, 0) if b == 0 else None)
    corner = moved(local, ("yh", "p"), lambda a, b: (1 - a, 1) if b == 0 else None)
    mine = jnp.where(p == 0, local, swapped)
    theirs = jnp.where(p == 0, across, corner)
    encoded = jnp.where(yh == 0, jnp.concatenate([mine, theirs]), jnp.concatenate([theirs, mine]))
    encoded = gathered(encoded, "x")
    decoding = jnp.where(p == 0, swapped[:128], local[128:])
    gain_rows = jnp.broadcast_to(final_gain[None], (16, 512))
    decoder_side = gathered(jnp.concatenate([decoding, gain_rows]), "x")

    full = decoder_side[:, :128].transpose(1, 0, 2).reshape(128, 2048).astype(f32)
    mean_square = jnp.mean(full * full, axis=-1, keepdims=True)
    query_in = full * lax.rsqrt(mean_square + epsilon) * decoder_gain.astype(f32)
    query = jnp.dot(query_in.astype(bf16), query_weight, preferred_element_type=f32).astype(bf16)

    terms = ffn(encoded, encoder_gain.reshape(4, 512), weights)
    terms = lax.all_to_all(terms.reshape(16, 32, 2048), PLANE, 0, 0)
    rows = lax.dynamic_slice_in_dim(encoded, ((yh * 2 + p) * 4 + x) * 32, 32, 1)
    memory = pl.pallas_call(
        memory_kernel,
        in_specs=[vmem()] * 3,
        out_specs=vmem(),
        out_shape=jax.ShapeDtypeStruct((4, 32, 2048), bf16),
        compiler_params=pltpu.CompilerParams(vmem_limit_bytes=16 * MIB),
    )(terms, rows, decoder_side[:, 128])
    memory = lax.all_to_all(memory, "x", 0, 0).reshape(128, 2048)

    attended = pl.pallas_call(
        attention_kernel,
        in_specs=[pl.BlockSpec(memory_space=pltpu.SMEM)] + [vmem()] * 5,
        out_specs=vmem(),
        out_shape=jax.ShapeDtypeStruct((4, 128, 512), bf16),
        compiler_params=pltpu.CompilerParams(vmem_limit_bytes=32 * MIB),
    )(
        lax.dynamic_slice_in_dim(lengths, p, 1, 0),
        query,
        memory,
        key_weight,
        value_weight,
        output_weight,
    )
    columns = lax.dynamic_slice_in_dim(memory, x * 512, 512, 1)
    later = moved(columns, ("p",), lambda a: (0,) if a == 1 else None)
    attended = lax.all_to_all(attended, "x", 0, 0)
    summed = jnp.sum(attended.astype(f32), axis=0)
    decoded = (decoding.astype(f32) + summed).astype(bf16)
    earlier = moved(decoded, ("p",), lambda a: (1,) if a == 0 else None)
    first = jnp.where(p == 0, columns, earlier)
    second = jnp.where(p == 0, later, decoded)
    return jnp.concatenate([first, second]).reshape(1, 2, 128, 512)


def solution(mesh):
    names = tuple(SIZES)
    fine = Mesh(mesh.devices.reshape(tuple(SIZES.values())), names)
    dp = ("yh", "z", "c")
    placed = (
        P("p", dp, None, "x"),
        P(dp),
        P(),
        P(dp, "x"),
        P(dp, "x"),
        P("x", dp),
        P("x"),
        P(),
        P(None, "x"),
        P(None, "x"),
        P(None, "x"),
        P("x", None),
    )
    return jax.shard_map(
        shards, mesh=fine, in_specs=placed, out_specs=P("p", dp, None, "x"), check_vma=False
    )
```

```python
import jax
import jax.numpy as jnp
import numpy as np
from jax import lax
from jax.experimental import pallas as pl
from jax.experimental.pallas import tpu as pltpu
from jax.sharding import Mesh, PartitionSpec as P

HEAD_DIM = 256
epsilon = 1e-06
SIZES = {"yh": 2, "z": 8, "c": 2, "p": 2, "x": 4}
LINE = ("z", "c")
bf16, f32 = jnp.bfloat16, jnp.float32
MIB = 1 << 20


def moved(value, axes, route):
    dims = [SIZES[a] for a in axes]
    pairs = []
    for at in np.ndindex(*dims):
        to = route(*at)
        if to is not None:
            pairs.append((int(np.ravel_multi_index(at, dims)), int(np.ravel_multi_index(to, dims))))
    return lax.ppermute(value, axes, pairs)


def gathered(value, axis):
    spread = jnp.broadcast_to(value[None], (SIZES[axis],) + value.shape)
    return lax.all_to_all(spread, axis, 0, 0)


def over(value, way):
    return moved(value, ("yh", "p"), lambda a, b: (a ^ (way // 2), b ^ (way % 2)))


def whole(shape):
    return pl.BlockSpec(shape, lambda *_: (0,) * len(shape))


def ffn_kernel(place, tokens, gain, weights, left, *rest):
    right, tile = rest[:4], rest[4]
    square = 0.0
    for b in range(4):
        t = tokens[b].astype(f32)
        square = square + jnp.sum(t * t, axis=-1, keepdims=True)
    scale = lax.rsqrt(square * (1.0 / 2048) + epsilon)
    gate = lift = 0.0
    for yh in range(2):
        for zz in range(4):
            b, at = yh * 2 + zz // 2, (zz % 2) * 256
            t = tokens[b, :, at : at + 256].astype(f32)
            n = (t * scale * gain[b : b + 1, at : at + 256].astype(f32)).astype(bf16)
            parts = [[weights[zz * 4 + k, yh, m] for k in range(4)] for m in range(2)]
            gate += jnp.dot(n, jnp.concatenate(parts[0], 0), preferred_element_type=f32)
            lift += jnp.dot(n, jnp.concatenate(parts[1], 0), preferred_element_type=f32)
    inner = 0.7978845608028654 * (gate + 0.044715 * (gate * gate * gate))
    hidden = (0.5 * gate * (1.0 + jnp.tanh(inner)) * lift).astype(bf16)
    for yh in range(2):
        for zz in range(4):
            half, at = zz // 2, (zz % 2) * 256
            down = jnp.concatenate([weights[zz * 4 + k, yh, 2] for k in range(4)], 0)
            part = lax.dot_general(hidden, down, (((1,), (1,)), ((), ())), preferred_element_type=f32)
            part = part.astype(bf16)
            for p in range(2):
                for x in range(4):
                    rows = part[(p * 4 + x) * 32 : (p * 4 + x + 1) * 32]
                    if yh == 0:
                        left[x, p, half, :, at : at + 256] = rows
                    else:
                        tile[p, x, half, :, at : at + 256] = rows
    for way in range(4):

        @pl.when(pl.program_id(0) == place[0] ^ (way // 2))
        def _():
            right[way][...] = tile[place[1] ^ (way % 2)]


def ffn(place, tokens, gain, weights):
    rows = tokens.shape[1]
    return pl.pallas_call(
        ffn_kernel,
        grid=(2,),
        in_specs=[
            pl.BlockSpec(memory_space=pltpu.SMEM),
            pl.BlockSpec((4, 256, 512), lambda i: (0, i, 0)),
            whole(gain.shape),
            whole(weights.shape),
        ],
        out_specs=[pl.BlockSpec((4, 2, 2, 32, 512), lambda i: (0, i, 0, 0, 0))]
        + [whole((4, 2, 32, 512))] * 4,
        out_shape=[jax.ShapeDtypeStruct((4, 4, 2, 32, 512), bf16)]
        + [jax.ShapeDtypeStruct((4, 2, 32, 512), bf16)] * 4,
        scratch_shapes=[pltpu.VMEM((2, 4, 2, 32, 512), bf16)],
        compiler_params=pltpu.CompilerParams(vmem_limit_bytes=48 * MIB),
        cost_estimate=pl.CostEstimate(
            flops=rows * 2048 * 512 * 6, bytes_accessed=10 * MIB, transcendentals=rows * 512
        ),
    )(place, tokens, gain, weights)


def added(refs):
    total = refs[0].astype(f32)
    for value in refs[1:]:
        total = total + value.astype(f32)
    return total


def between_kernel(place, left, r0, r1, r2, r3, o0, o1, o2, o3, right):
    for way, out in enumerate((o0, o1, o2, o3)):
        to = (place[0] * 2 + place[1]) ^ way
        out[...] = added([left[k, to] for k in range(4)]).astype(bf16)
    for x in range(4):
        right[x] = added([r[x] for r in (r0, r1, r2, r3)]).astype(bf16)


def memory_kernel(l0, l1, l2, l3, right, tokens, gain, out):
    square, kept = 0.0, []
    for b in range(4):
        if b < 2:
            total = added([r[b] for r in (l0, l1, l2, l3)])
        else:
            total = added([right[k, b - 2] for k in range(4)])
        merged = tokens[b].astype(f32) + total
        square = square + jnp.sum(merged * merged, axis=-1, keepdims=True)
        kept.append(merged)
    scale = lax.rsqrt(square * (1.0 / 2048) + epsilon)
    for b in range(4):
        at = slice(b * 512, (b + 1) * 512)
        rounded = (kept[b] * scale * gain[b : b + 1].astype(f32)).astype(bf16)
        for k in range(4):
            out[k, :, at] = rounded


def prepare_kernel(tokens, gain, after, wq, wk, wv, wo, query, key_out, value_out, output_out, sems):
    copies = [
        pltpu.make_async_copy(src, dst, sems.at[i])
        for i, (src, dst) in enumerate(((wk, key_out), (wv, value_out), (wo, output_out)))
    ]
    for copy in copies:
        copy.start()
    square = 0.0
    for b in range(4):
        t = tokens[b].astype(f32)
        square = square + jnp.sum(t * t, axis=-1, keepdims=True)
    scale = lax.rsqrt(square * (1.0 / 2048) + epsilon)
    total = 0.0
    for b in range(4):
        n = (tokens[b].astype(f32) * scale * gain[b : b + 1].astype(f32)).astype(bf16)
        total += jnp.dot(n, wq[b * 512 : (b + 1) * 512], preferred_element_type=f32)
    query[...] = total.astype(bf16)
    for copy in copies:
        copy.wait()


def attention_kernel(lengths, query, memory, key_weight, value_weight, output_weight, out):
    source = memory[...]
    keys = jnp.dot(source, key_weight[...], preferred_element_type=f32).astype(bf16)
    values = jnp.dot(source, value_weight[...], preferred_element_type=f32).astype(bf16)
    positions = lax.broadcasted_iota(jnp.int32, (128, 128), 1)
    valid = positions < lengths[0]
    contexts = []
    for h in range(2):
        at = slice(h * HEAD_DIM, (h + 1) * HEAD_DIM)
        scores = lax.dot_general(
            query[:, at], keys[:, at], (((1,), (1,)), ((), ())), preferred_element_type=f32
        )
        scores = jnp.where(valid, scores, -1e30)
        weights = jnp.exp(scores - jnp.max(scores, axis=-1, keepdims=True))
        probs = (weights / jnp.sum(weights, axis=-1, keepdims=True)).astype(bf16)
        contexts.append(jnp.dot(probs, values[:, at], preferred_element_type=f32).astype(bf16))
    context = jnp.concatenate(contexts, axis=1)
    for b in range(4):
        part = jnp.dot(
            context, output_weight[:, b * 512 : (b + 1) * 512], preferred_element_type=f32
        )
        out[b] = part.astype(bf16)


def vmem():
    return pl.BlockSpec(memory_space=pltpu.VMEM)


def shards(
    streams,
    lengths,
    encoder_gain,
    ffn_gate,
    ffn_lift,
    ffn_down,
    final_gain,
    decoder_gain,
    query_weight,
    key_weight,
    value_weight,
    output_weight,
):
    yh, p, x = lax.axis_index("yh"), lax.axis_index("p"), lax.axis_index("x")
    local = streams[0].reshape(256, 512)

    stack = jnp.stack([ffn_gate, ffn_lift, ffn_down.T])

    def quarter(at):
        return lax.dynamic_slice_in_dim(stack, (p * 2 + at) * 512, 512, 2)

    own = quarter(yh)
    other = moved(quarter(1 - yh), ("yh",), lambda a: (1 - a,))
    both = jnp.where(yh == 0, jnp.stack([own, other]), jnp.stack([other, own]))
    weights = lax.all_gather(both, LINE, axis=0)

    swapped = moved(local, ("p",), lambda a: (1 - a,))
    across = moved(local, ("yh", "p"), lambda a, b: (1 - a, 0) if b == 0 else None)
    corner = moved(local, ("yh", "p"), lambda a, b: (1 - a, 1) if b == 0 else None)
    mine = jnp.where(p == 0, local, swapped)
    theirs = jnp.where(p == 0, across, corner)
    encoded = jnp.where(yh == 0, jnp.concatenate([mine, theirs]), jnp.concatenate([theirs, mine]))
    encoded = gathered(encoded, "x")
    decoding = jnp.where(p == 0, swapped[:128], local[128:])
    gain_rows = jnp.broadcast_to(final_gain[None], (16, 512))
    decoder_side = gathered(jnp.concatenate([decoding, gain_rows]), "x")

    place = jnp.stack([yh, p, x]).astype(jnp.int32)
    left, *right = ffn(place, encoded, encoder_gain.reshape(4, 512), weights)
    left = lax.all_to_all(left, "x", 0, 0)
    right = [right[0]] + [over(right[way], way) for way in (1, 2, 3)]
    *left, right = pl.pallas_call(
        between_kernel,
        in_specs=[pl.BlockSpec(memory_space=pltpu.SMEM)] + [vmem()] * 5,
        out_specs=[vmem()] * 5,
        out_shape=[jax.ShapeDtypeStruct((2, 32, 512), bf16)] * 4
        + [jax.ShapeDtypeStruct((4, 2, 32, 512), bf16)],
        compiler_params=pltpu.CompilerParams(vmem_limit_bytes=16 * MIB),
    )(place, left, *right)
    rows = lax.dynamic_slice_in_dim(encoded, ((yh * 2 + p) * 4 + x) * 32, 32, 1)
    left = [left[0]] + [over(left[way], way) for way in (1, 2, 3)]
    right = lax.all_to_all(right, "x", 0, 0)
    memory = pl.pallas_call(
        memory_kernel,
        in_specs=[vmem()] * 7,
        out_specs=vmem(),
        out_shape=jax.ShapeDtypeStruct((4, 32, 2048), bf16),
        compiler_params=pltpu.CompilerParams(vmem_limit_bytes=16 * MIB),
    )(*left, right, rows, decoder_side[:, 128])
    anyplace = pl.BlockSpec(memory_space=pl.ANY)
    prepared = pl.pallas_call(
        prepare_kernel,
        in_specs=[vmem()] * 2 + [anyplace, vmem()] + [anyplace] * 3,
        out_specs=[vmem()] * 4,
        out_shape=[jax.ShapeDtypeStruct((128, 512), bf16)]
        + [jax.ShapeDtypeStruct(w.shape, bf16) for w in (key_weight, value_weight, output_weight)],
        scratch_shapes=[pltpu.SemaphoreType.DMA((3,))],
        compiler_params=pltpu.CompilerParams(vmem_limit_bytes=16 * MIB),
        cost_estimate=pl.CostEstimate(
            flops=2 * 128 * 2048 * 512, bytes_accessed=14 * MIB, transcendentals=0
        ),
    )(
        decoder_side[:, :128],
        decoder_gain.reshape(4, 512),
        memory,
        query_weight,
        key_weight,
        value_weight,
        output_weight,
    )
    memory = lax.all_to_all(memory, "x", 0, 0).reshape(128, 2048)

    attended = pl.pallas_call(
        attention_kernel,
        in_specs=[pl.BlockSpec(memory_space=pltpu.SMEM)] + [vmem()] * 5,
        out_specs=vmem(),
        out_shape=jax.ShapeDtypeStruct((4, 128, 512), bf16),
        compiler_params=pltpu.CompilerParams(vmem_limit_bytes=16 * MIB),
        cost_estimate=pl.CostEstimate(
            flops=6 * 128 * 2048 * 512, bytes_accessed=10 * MIB, transcendentals=0
        ),
    )(lax.dynamic_slice_in_dim(lengths, p, 1, 0), prepared[0], memory, *prepared[1:])
    columns = lax.dynamic_slice_in_dim(memory, x * 512, 512, 1)
    attended = lax.all_to_all(attended, "x", 0, 0)
    summed = jnp.sum(attended.astype(f32), axis=0)
    decoded = (decoding.astype(f32) + summed).astype(bf16)
    swapped = moved(jnp.where(p == 0, decoded, columns), ("p",), lambda a: (1 - a,))
    kept = jnp.where(p == 0, columns, decoded)
    first, second = jnp.where(p == 0, kept, swapped), jnp.where(p == 0, swapped, kept)
    return jnp.concatenate([first, second]).reshape(1, 2, 128, 512)


def solution(mesh):
    names = tuple(SIZES)
    fine = Mesh(mesh.devices.reshape(tuple(SIZES.values())), names)
    dp = ("yh", "z", "c")
    placed = (
        P("p", dp, None, "x"),
        P(dp),
        P(),
        P(dp, "x"),
        P(dp, "x"),
        P("x", dp),
        P("x"),
        P(),
        P(None, "x"),
        P(None, "x"),
        P(None, "x"),
        P("x", None),
    )
    return jax.shard_map(
        shards, mesh=fine, in_specs=placed, out_specs=P("p", dp, None, "x"), check_vma=False
    )
```

```python
import jax
import jax.numpy as jnp
import numpy as np
from jax import lax
from jax.experimental import pallas as pl
from jax.experimental.pallas import tpu as pltpu
from jax.sharding import Mesh, PartitionSpec as P

HEAD_DIM = 256
epsilon = 1e-06
SIZES = {"yh": 2, "z": 8, "c": 2, "p": 2, "x": 4}
PLANE = ("yh", "p", "x")
bf16, f32 = jnp.bfloat16, jnp.float32
MIB = 1 << 20


def moved(value, axes, route):
    dims = [SIZES[a] for a in axes]
    pairs = []
    for at in np.ndindex(*dims):
        to = route(*at)
        if to is not None:
            pairs.append((int(np.ravel_multi_index(at, dims)), int(np.ravel_multi_index(to, dims))))
    return lax.ppermute(value, axes, pairs)


def passed(value):
    return moved(
        value, ("z", "c"), lambda z, c: ((z + 1) % 8, c) if c == 0 else ((z - 1) % 8, c)
    )


def after(value, *others):
    def kernel(*refs):
        del refs

    return pl.pallas_call(
        kernel,
        in_specs=[anyplace()] * (1 + len(others)),
        out_specs=anyplace(),
        out_shape=jax.ShapeDtypeStruct(value.shape, value.dtype),
        input_output_aliases={0: 0},
        compiler_params=params(),
    )(value, *others)


def gather_lines(near, far, *ready):
    near, far = [near], [far]
    for k in range(3):
        near.append(after(passed(near[k]), *ready[k]))
        far.append(passed(far[k]))
    near.append(passed(near[3][:192]))
    far.append(passed(far[3][:192]))
    return [v for line in (near, far) for v in line + [twin(chunk) for chunk in line[1:]]]


def opposite(value):
    return moved(value, ("yh", "p"), lambda a, b: (1 - a, 1 - b))


def around(value):
    return [value] + [moved(value, ("x",), lambda a: ((a + k) % 4,)) for k in (1, 2, 3)]


def twin(value):
    return moved(value, ("c",), lambda a: (1 - a,))


def whole(shape):
    return pl.BlockSpec(shape, lambda *_: (0,) * len(shape))


def params(mib=60):
    return pltpu.CompilerParams(vmem_limit_bytes=mib * MIB)


def smem():
    return pl.BlockSpec(memory_space=pltpu.SMEM)


def vmem():
    return pl.BlockSpec(memory_space=pltpu.VMEM)


def anyplace():
    return pl.BlockSpec(memory_space=pl.ANY)


CHUNKS = 9


def normed_block(block, scale, gain):
    return (block[...].astype(f32) * scale * gain.astype(f32)).astype(bf16)


def scale_of(blocks):
    square = 0.0
    for block in blocks:
        t = block[...].astype(f32)
        square = square + jnp.sum(t * t, axis=-1, keepdims=True)
    return lax.rsqrt(square * (1.0 / 2048) + epsilon)


def ffn_kernel(place, *refs):
    tokens, gain, refs = refs[:8], refs[8], refs[9:]
    chunks, (out, held, normed, sems) = refs[: 2 * CHUNKS], refs[2 * CHUNKS :]
    yh, x, z, c = place[0], place[2], place[3], place[4]
    first = pl.program_id(0) == 0
    ways = [(m, side) for side in range(2) for m in range(2)] + [(2, 0), (2, 1)]

    @pl.when(first)
    def _():
        for m, side in ways:
            for k in range(CHUNKS):
                chunk = chunks[side * CHUNKS + k]
                step, core = (k, c) if k < 5 else (k - 4, 1 - c)
                at = (z - step * (1 - 2 * core)) & 7
                for half in range(chunk.shape[0] // 192):
                    source = chunk.at[pl.ds(half * 192 + m * 64, 64)]
                    target = held.at[m, side, at, core ^ half]
                    pltpu.make_async_copy(source, target, sems.at[m, side]).start()

    def wait(*those):
        @pl.when(first)
        def _():
            for spot in those:
                pltpu.make_async_copy(held.at[spot], held.at[spot], sems.at[spot]).wait()

    for i in range(2):

        @pl.when(pl.program_id(0) == i)
        def _():
            blocks = tokens[i * 4 : (i + 1) * 4]
            scale = scale_of(blocks)
            for k, block in enumerate(blocks):
                b = (x - k) & 3
                normed[b] = normed_block(block, scale, gain[b])

    gate = lift = 0.0
    for side in range(2):
        b = (yh ^ side) * 2
        n = jnp.concatenate([normed[b], normed[b + 1]], 1)
        wait((0, side), (1, side))
        gate += jnp.dot(n, held[0, side].reshape(1024, 512), preferred_element_type=f32)
        lift += jnp.dot(n, held[1, side].reshape(1024, 512), preferred_element_type=f32)
    inner = 0.7978845608028654 * (gate + 0.044715 * (gate * gate * gate))
    hidden = (0.5 * gate * (1.0 + jnp.tanh(inner)) * lift).astype(bf16)
    wait((2, 0), (2, 1))
    for side in range(2):
        for k in range(2):
            rows = held[2, side, k * 4 : (k + 1) * 4].reshape(512, 512)
            part = lax.dot_general(
                hidden, rows, (((1,), (1,)), ((), ())), preferred_element_type=f32
            )
            out[:, (yh ^ side) * 2 + k] = part.astype(bf16).reshape(8, 32, 512)


def ffn(place, tokens, gain, chunks):
    grid_spec = pltpu.PrefetchScalarGridSpec(
        num_scalar_prefetch=1,
        grid=(2,),
        in_specs=[pl.BlockSpec((256, 512), lambda i, place: (0, 0))] * 8
        + [whole(gain.shape)]
        + [anyplace()] * len(chunks),
        out_specs=pl.BlockSpec((8, 4, 32, 512), lambda i, place: (place[0] ^ i, 0, 0, 0)),
        scratch_shapes=[
            pltpu.VMEM((3, 2, 8, 2, 64, 512), bf16),
            pltpu.VMEM((4, 256, 512), bf16),
            pltpu.SemaphoreType.DMA((3, 2)),
        ],
    )
    return pl.pallas_call(
        ffn_kernel,
        grid_spec=grid_spec,
        out_shape=jax.ShapeDtypeStruct((16, 4, 32, 512), bf16),
        compiler_params=params(),
        cost_estimate=pl.CostEstimate(
            flops=512 * 2048 * 512 * 6, bytes_accessed=10 * MIB, transcendentals=512 * 512
        ),
    )(place, *tokens, gain, *chunks)


def memory_kernel(place, terms, tokens, gain, out):
    square, kept = 0.0, []
    for i in range(4):
        b = (place[2] - i) & 3
        total = terms[0, b].astype(f32)
        for k in range(1, 16):
            total = total + terms[k, b].astype(f32)
        merged = tokens[i].astype(f32) + total
        square = square + jnp.sum(merged * merged, axis=-1, keepdims=True)
        kept.append(merged)
    scale = lax.rsqrt(square * (1.0 / 2048) + epsilon)
    for i in range(4):
        at = pl.ds(pl.multiple_of(((place[2] - i) & 3) * 512, 512), 512)
        rounded = (kept[i] * scale * gain[i : i + 1].astype(f32)).astype(bf16)
        for k in range(4):
            out[k, :, at] = rounded


def memory_rows(place, terms, tokens, gain):
    return pl.pallas_call(
        memory_kernel,
        in_specs=[smem()] + [vmem()] * 3,
        out_specs=vmem(),
        out_shape=jax.ShapeDtypeStruct((4, 32, 2048), bf16),
        compiler_params=params(16),
    )(place, terms, tokens, gain)


def query_kernel(place, t0, t1, t2, t3, gain, weight, out):
    blocks = (t0, t1, t2, t3)
    scale = scale_of(blocks)
    total = 0.0
    for k, block in enumerate(blocks):
        b = (place[2] - k) & 3
        rows = weight[pl.ds(pl.multiple_of(b * 512, 512), 512), :]
        n = normed_block(block, scale, gain[b])
        total += jnp.dot(n, rows, preferred_element_type=f32)
    out[...] = total.astype(bf16)


def query_rows(place, tokens, gain, weight):
    grid_spec = pltpu.PrefetchScalarGridSpec(
        num_scalar_prefetch=1,
        grid=(1,),
        in_specs=[pl.BlockSpec((128, 512), lambda i, place: (2, 0))] * 4
        + [whole(gain.shape), whole(weight.shape)],
        out_specs=whole((128, 512)),
    )
    return pl.pallas_call(
        query_kernel,
        grid_spec=grid_spec,
        out_shape=jax.ShapeDtypeStruct((128, 512), bf16),
        compiler_params=params(),
        cost_estimate=pl.CostEstimate(
            flops=2 * 128 * 2048 * 512, bytes_accessed=3 * MIB, transcendentals=0
        ),
    )(place, *tokens, gain, weight)


def attention_kernel(place, lengths, query, memory, wk, wv, wo, out, columns, held, sems):
    held_in, held_out = held
    columns[...] = memory[:, pl.ds(pl.multiple_of(place[2] * 512, 512), 512)]
    copies = []
    for k in range(8):
        source = (wk, wv)[k // 4].at[pl.ds((k % 4) * 512, 512)]
        copies.append(pltpu.make_async_copy(source, held_in.at[k], sems.at[k]))
    for k in range(2):
        rows = pl.ds(k * 256, 256)
        copies.append(pltpu.make_async_copy(wo.at[rows], held_out.at[rows], sems.at[8 + k]))
    for copy in copies:
        copy.start()
    made = []
    for m in range(2):
        total = 0.0
        for k in range(4):
            copies[m * 4 + k].wait()
            total += jnp.dot(
                memory[:, k * 512 : (k + 1) * 512], held_in[m * 4 + k], preferred_element_type=f32
            )
        made.append(total.astype(bf16))
    keys, values = made
    positions = lax.broadcasted_iota(jnp.int32, (128, 128), 1)
    valid = positions < lengths[place[1]]
    contexts = []
    for h in range(2):
        at = slice(h * HEAD_DIM, (h + 1) * HEAD_DIM)
        scores = lax.dot_general(
            query[:, at], keys[:, at], (((1,), (1,)), ((), ())), preferred_element_type=f32
        )
        scores = jnp.where(valid, scores, -1e30)
        weights = jnp.exp(scores - jnp.max(scores, axis=-1, keepdims=True))
        probs = (weights / jnp.sum(weights, axis=-1, keepdims=True)).astype(bf16)
        contexts.append(jnp.dot(probs, values[:, at], preferred_element_type=f32).astype(bf16))
    copies[8].wait()
    copies[9].wait()
    context = jnp.concatenate(contexts, axis=1)
    for b in range(4):
        part = jnp.dot(
            context, held_out[:, b * 512 : (b + 1) * 512], preferred_element_type=f32
        )
        out[b] = part.astype(bf16)


def attention(place, lengths, query, memory, wk, wv, wo):
    return pl.pallas_call(
        attention_kernel,
        in_specs=[smem()] * 2 + [vmem()] * 2 + [anyplace()] * 3,
        out_specs=[vmem()] * 2,
        out_shape=[
            jax.ShapeDtypeStruct((4, 128, 512), bf16),
            jax.ShapeDtypeStruct((128, 512), bf16),
        ],
        scratch_shapes=[
            (pltpu.VMEM((8, 512, 512), bf16), pltpu.VMEM((512, 2048), bf16)),
            pltpu.SemaphoreType.DMA((10,)),
        ],
        compiler_params=params(),
        cost_estimate=pl.CostEstimate(
            flops=6 * 128 * 2048 * 512, bytes_accessed=8 * MIB, transcendentals=128 * 256
        ),
    )(place, lengths, query, memory, wk, wv, wo)


def shards(
    streams,
    lengths,
    encoder_gain,
    ffn_gate,
    ffn_lift,
    ffn_down,
    final_gain,
    decoder_gain,
    query_weight,
    key_weight,
    value_weight,
    output_weight,
):
    place = jnp.stack([lax.axis_index(a) for a in ("yh", "p", "x", "z", "c")]).astype(jnp.int32)
    p, x = place[1], place[2]
    local = streams[0].reshape(256, 512)

    def quarter(yh, p):
        start = (p * 2 + yh) * 512
        return jnp.concatenate(
            [lax.dynamic_slice_in_dim(w, start, 512, 1) for w in (ffn_gate, ffn_lift, ffn_down.T)]
        )

    own, rest = quarter(place[0], p), opposite(quarter(1 - place[0], 1 - p))
    near, far = jnp.concatenate([own, twin(own)]), jnp.concatenate([rest, twin(rest)])

    swapped = moved(local, ("p",), lambda a: (1 - a,))
    mine = jnp.where(p == 0, local, swapped)
    theirs = opposite(mine)
    decoding = jnp.where(p == 0, swapped[:128], local[128:])
    gain_rows = jnp.broadcast_to(final_gain[None], (16, 512))
    tokens = around(jnp.concatenate([mine, decoding, gain_rows]))
    others = around(theirs)
    chunks = gather_lines(near, far, (swapped,), (theirs,), tokens[1:] + others[1:])

    terms = ffn(place, tokens + others, encoder_gain.reshape(4, 1, 512), chunks)
    terms = lax.all_to_all(terms, ("yh", "p", "x"), 0, 0)
    query = query_rows(place, tokens, decoder_gain.reshape(4, 1, 512), query_weight)
    rows = [lax.dynamic_slice_in_dim(t, (p * 4 + x) * 32, 32, 0) for t in tokens]
    gains = [t[384] for t in tokens]
    memory = memory_rows(place, terms, jnp.stack(rows), jnp.stack(gains))
    memory = lax.all_to_all(memory, "x", 0, 0).reshape(128, 2048)
    attended, columns = attention(
        place, lengths, query, memory, key_weight, value_weight, output_weight
    )
    attended = lax.all_to_all(attended, "x", 0, 0)
    summed = jnp.sum(attended.astype(f32), axis=0)
    decoded = (decoding.astype(f32) + summed).astype(bf16)
    swapped = moved(jnp.where(p == 0, decoded, columns), ("p",), lambda a: (1 - a,))
    first = jnp.where(p == 0, columns, swapped)
    second = jnp.where(p == 0, swapped, decoded)
    return jnp.concatenate([first, second]).reshape(1, 2, 128, 512)


def solution(mesh):
    names = tuple(SIZES)
    fine = Mesh(mesh.devices.reshape(tuple(SIZES.values())), names)
    dp = ("yh", "z", "c")
    placed = (
        P("p", dp, None, "x"),
        P(dp),
        P(),
        P(dp, "x"),
        P(dp, "x"),
        P("x", dp),
        P("x"),
        P(),
        P(None, "x"),
        P(None, "x"),
        P(None, "x"),
        P("x", None),
    )
    return jax.shard_map(
        shards, mesh=fine, in_specs=placed, out_specs=P("p", dp, None, "x"), check_vma=False
    )
```

```python
import jax
import jax.numpy as jnp
import numpy as np
from jax import lax
from jax.experimental import pallas as pl
from jax.experimental.pallas import tpu as pltpu
from jax.sharding import Mesh, PartitionSpec as P

HEAD_DIM = 256
epsilon = 1e-06
SIZES = {"yh": 2, "z": 8, "c": 2, "p": 2, "x": 4}
PLANE = ("yh", "p", "x")
bf16, f32 = jnp.bfloat16, jnp.float32
MIB = 1 << 20


def moved(value, axes, route):
    dims = [SIZES[a] for a in axes]
    pairs = []
    for at in np.ndindex(*dims):
        to = route(*at)
        if to is not None:
            pairs.append((int(np.ravel_multi_index(at, dims)), int(np.ravel_multi_index(to, dims))))
    return lax.ppermute(value, axes, pairs)


def passed(value):
    return moved(
        value, ("z", "c"), lambda z, c: ((z + 1) % 8, c) if c == 0 else ((z - 1) % 8, c)
    )


def after(value, *others):
    if not others:
        return value

    def kernel(*refs):
        del refs

    return pl.pallas_call(
        kernel,
        in_specs=[anyplace()] * (1 + len(others)),
        out_specs=anyplace(),
        out_shape=jax.ShapeDtypeStruct(value.shape, value.dtype),
        input_output_aliases={0: 0},
        compiler_params=params(),
    )(value, *others)


def gather_lines(near, far, ready):
    near, far = [near], [far]
    for k in range(3):
        near.append(after(passed(near[k]), *ready[k]))
        far.append(passed(far[k]))
    near.append(after(passed(near[3][:192]), *ready[3]))
    far.append(passed(far[3][:192]))
    return [v for line in (near, far) for v in line + [twin(chunk) for chunk in line[1:]]]


def opposite(value):
    return moved(value, ("yh", "p"), lambda a, b: (1 - a, 1 - b))


def shifted(value, k):
    return moved(value, ("x",), lambda a: ((a + k) % 4,)) if k else value


def around(value, cut):
    up, down = (lambda a: ((a + 1) % 4,)), (lambda a: ((a - 1) % 4,))
    first, third = moved(value, ("x",), up), moved(value, ("x",), down)
    second = moved(first[:cut], ("x",), up), moved(third[cut:], ("x",), down)
    return value, first, second, third


def twin(value):
    return moved(value, ("c",), lambda a: (1 - a,))


def whole(shape):
    return pl.BlockSpec(shape, lambda *_: (0,) * len(shape))


def params(mib=60):
    return pltpu.CompilerParams(vmem_limit_bytes=mib * MIB)


def smem():
    return pl.BlockSpec(memory_space=pltpu.SMEM)


def vmem():
    return pl.BlockSpec(memory_space=pltpu.VMEM)


def anyplace():
    return pl.BlockSpec(memory_space=pl.ANY)


CHUNKS = 9


def normed_block(block, scale, gain):
    return (block[...].astype(f32) * scale * gain.astype(f32)).astype(bf16)


def scale_of(blocks):
    square = 0.0
    for block in blocks:
        t = block[...].astype(f32)
        square = square + jnp.sum(t * t, axis=-1, keepdims=True)
    return lax.rsqrt(square * (1.0 / 2048) + epsilon)


def ffn_kernel(place, *refs):
    tokens, gain, refs = refs[:8], refs[8], refs[9:]
    chunks, (out, held, normed, sems) = refs[: 2 * CHUNKS], refs[2 * CHUNKS :]
    yh, x, z, c = place[0], place[2], place[3], place[4]
    first = pl.program_id(0) == 0
    ways = [(m, side) for side in range(2) for m in range(2)] + [(2, 0), (2, 1)]

    @pl.when(first)
    def _():
        for m, side in ways:
            for k in range(CHUNKS):
                chunk = chunks[side * CHUNKS + k]
                step, core = (k, c) if k < 5 else (k - 4, 1 - c)
                at = (z - step * (1 - 2 * core)) & 7
                for half in range(chunk.shape[0] // 192):
                    source = chunk.at[pl.ds(half * 192 + m * 64, 64)]
                    target = held.at[m, side, at, core ^ half]
                    pltpu.make_async_copy(source, target, sems.at[m, side]).start()

    def wait(*those):
        @pl.when(first)
        def _():
            for spot in those:
                pltpu.make_async_copy(held.at[spot], held.at[spot], sems.at[spot]).wait()

    for i in range(2):

        @pl.when(pl.program_id(0) == i)
        def _():
            blocks = tokens[i * 4 : (i + 1) * 4]
            scale = scale_of(blocks)
            for k, block in enumerate(blocks):
                b = (x - k) & 3
                normed[b] = normed_block(block, scale, gain[b])

    gate = lift = 0.0
    for side in range(2):
        b = (yh ^ side) * 2
        n = jnp.concatenate([normed[b], normed[b + 1]], 1)
        wait((0, side), (1, side))
        gate += jnp.dot(n, held[0, side].reshape(1024, 512), preferred_element_type=f32)
        lift += jnp.dot(n, held[1, side].reshape(1024, 512), preferred_element_type=f32)
    inner = 0.7978845608028654 * (gate + 0.044715 * (gate * gate * gate))
    hidden = (0.5 * gate * (1.0 + jnp.tanh(inner)) * lift).astype(bf16)
    wait((2, 0), (2, 1))
    for side in range(2):
        for k in range(2):
            rows = held[2, side, k * 4 : (k + 1) * 4].reshape(512, 512)
            part = lax.dot_general(
                hidden, rows, (((1,), (1,)), ((), ())), preferred_element_type=f32
            )
            out[:, (yh ^ side) * 2 + k] = part.astype(bf16).reshape(8, 32, 512)


def rows_at(rows, at):
    return pl.BlockSpec((rows, 512), lambda i, place: (at, 0))


def ffn(place, tokens, gain, chunks):
    first, second, (third, third_rest), fourth = tokens
    mine, theirs = (first, second, third, fourth), (first, second, third_rest, fourth)
    grid_spec = pltpu.PrefetchScalarGridSpec(
        num_scalar_prefetch=1,
        grid=(2,),
        in_specs=[rows_at(256, at) for at in (0, 0, 0, 0, 1, 1, 0, 1)]
        + [whole(gain.shape)]
        + [anyplace()] * len(chunks),
        out_specs=pl.BlockSpec((8, 4, 32, 512), lambda i, place: (place[0] ^ i, 0, 0, 0)),
        scratch_shapes=[
            pltpu.VMEM((3, 2, 8, 2, 64, 512), bf16),
            pltpu.VMEM((4, 256, 512), bf16),
            pltpu.SemaphoreType.DMA((3, 2)),
        ],
    )
    return pl.pallas_call(
        ffn_kernel,
        grid_spec=grid_spec,
        out_shape=jax.ShapeDtypeStruct((16, 4, 32, 512), bf16),
        compiler_params=params(),
        cost_estimate=pl.CostEstimate(
            flops=512 * 2048 * 512 * 6, bytes_accessed=10 * MIB, transcendentals=512 * 512
        ),
    )(place, *mine, *theirs, gain, *chunks)


def memory_kernel(place, terms, *refs):
    tokens, gains, out = refs[:4], refs[4:8], refs[8]
    square, kept = 0.0, []
    for i in range(4):
        b = (place[2] - i) & 3
        total = terms[0, b].astype(f32)
        for k in range(1, 16):
            total = total + terms[k, b].astype(f32)
        merged = tokens[i][...].astype(f32) + total
        square = square + jnp.sum(merged * merged, axis=-1, keepdims=True)
        kept.append(merged)
    scale = lax.rsqrt(square * (1.0 / 2048) + epsilon)
    for i in range(4):
        at = pl.ds(pl.multiple_of(((place[2] - i) & 3) * 512, 512), 512)
        rounded = (kept[i] * scale * gains[i][:1].astype(f32)).astype(bf16)
        out[:, at] = rounded


def memory_rows(place, terms, tokens):
    first, second, (third, third_rest), fourth = tokens
    grid_spec = pltpu.PrefetchScalarGridSpec(
        num_scalar_prefetch=1,
        grid=(1,),
        in_specs=[whole(terms.shape)]
        + [pl.BlockSpec((32, 512), lambda i, place: (place[1] * 4 + place[2], 0))] * 4
        + [rows_at(16, at) for at in (40, 40, 24, 40)],
        out_specs=whole((32, 2048)),
    )
    return pl.pallas_call(
        memory_kernel,
        grid_spec=grid_spec,
        out_shape=jax.ShapeDtypeStruct((32, 2048), bf16),
        compiler_params=params(16),
    )(place, terms, first, second, third, fourth, first, second, third_rest, fourth)


def query_kernel(place, t0, t1, t2, t3, gain, weight, out):
    blocks = (t0, t1, t2, t3)
    scale = scale_of(blocks)
    total = 0.0
    for k, block in enumerate(blocks):
        b = (place[2] - k) & 3
        rows = weight[pl.ds(pl.multiple_of(b * 512, 512), 512), :]
        n = normed_block(block, scale, gain[b])
        total += jnp.dot(n, rows, preferred_element_type=f32)
    out[...] = total.astype(bf16)


def query_rows(place, tokens, gain, weight):
    grid_spec = pltpu.PrefetchScalarGridSpec(
        num_scalar_prefetch=1,
        grid=(1,),
        in_specs=[rows_at(128, at) for at in (4, 4, 2, 4)]
        + [whole(gain.shape), whole(weight.shape)],
        out_specs=whole((128, 512)),
    )
    return pl.pallas_call(
        query_kernel,
        grid_spec=grid_spec,
        out_shape=jax.ShapeDtypeStruct((128, 512), bf16),
        compiler_params=params(),
        cost_estimate=pl.CostEstimate(
            flops=2 * 128 * 2048 * 512, bytes_accessed=3 * MIB, transcendentals=0
        ),
    )(place, tokens[0], tokens[1], tokens[2][1], tokens[3], gain, weight)


def attention_kernel(place, lengths, query, m0, m1, m2, m3, wk, wv, wo, *refs):
    outs, columns, held_in, held_out, sems = refs[:4], *refs[4:]
    x = place[2]
    copies = []
    for k in range(8):
        source = (wk, wv)[k // 4].at[pl.ds((k % 4) * 512, 512)]
        copies.append(pltpu.make_async_copy(source, held_in.at[k], sems.at[k]))
    for k in range(2):
        rows = pl.ds(k * 256, 256)
        copies.append(pltpu.make_async_copy(wo.at[rows], held_out.at[rows], sems.at[8 + k]))
    for copy in copies:
        copy.start()
    blocks = (m0, m1, m2, m3)
    mine = pl.ds(pl.multiple_of(x * 512, 512), 512)
    for k, block in enumerate(blocks):
        columns[pl.ds(pl.multiple_of(((x - k) & 3) * 32, 32), 32), :] = block[:, mine]
    memory = jnp.concatenate([block[...] for block in blocks], 0)
    made = []
    for m in range(2):
        total = 0.0
        for k in range(4):
            copies[m * 4 + k].wait()
            total += jnp.dot(
                memory[:, k * 512 : (k + 1) * 512], held_in[m * 4 + k], preferred_element_type=f32
            )
        made.append(total.astype(bf16))
    keys, values = made
    spots = lax.broadcasted_iota(jnp.int32, (128, 128), 1)
    positions = (((x - (spots >> 5)) & 3) << 5) + (spots & 31)
    valid = positions < lengths[place[1]]
    contexts = []
    for h in range(2):
        at = slice(h * HEAD_DIM, (h + 1) * HEAD_DIM)
        scores = lax.dot_general(
            query[:, at], keys[:, at], (((1,), (1,)), ((), ())), preferred_element_type=f32
        )
        scores = jnp.where(valid, scores, -1e30)
        weights = jnp.exp(scores - jnp.max(scores, axis=-1, keepdims=True))
        probs = (weights / jnp.sum(weights, axis=-1, keepdims=True)).astype(bf16)
        contexts.append(jnp.dot(probs, values[:, at], preferred_element_type=f32).astype(bf16))
    copies[8].wait()
    copies[9].wait()
    context = jnp.concatenate(contexts, axis=1)
    for k in range(4):
        at = pl.ds(pl.multiple_of(((x + k) & 3) * 512, 512), 512)
        part = jnp.dot(context, held_out[:, at], preferred_element_type=f32)
        outs[k][...] = part.astype(bf16)


def attention(place, lengths, query, memory, wk, wv, wo):
    return pl.pallas_call(
        attention_kernel,
        in_specs=[smem()] * 2 + [vmem()] * 5 + [anyplace()] * 3,
        out_specs=[vmem()] * 5,
        out_shape=[jax.ShapeDtypeStruct((128, 512), bf16)] * 5,
        scratch_shapes=[
            pltpu.VMEM((8, 512, 512), bf16),
            pltpu.VMEM((512, 2048), bf16),
            pltpu.SemaphoreType.DMA((10,)),
        ],
        compiler_params=params(),
        cost_estimate=pl.CostEstimate(
            flops=6 * 128 * 2048 * 512, bytes_accessed=8 * MIB, transcendentals=128 * 256
        ),
    )(place, lengths, query, *memory, wk, wv, wo)


def shards(
    streams,
    lengths,
    encoder_gain,
    ffn_gate,
    ffn_lift,
    ffn_down,
    final_gain,
    decoder_gain,
    query_weight,
    key_weight,
    value_weight,
    output_weight,
):
    place = jnp.stack([lax.axis_index(a) for a in ("yh", "p", "x", "z", "c")]).astype(jnp.int32)
    p, x = place[1], place[2]
    local = streams[0].reshape(256, 512)

    def quarter(yh, p):
        start = (p * 2 + yh) * 512
        return jnp.concatenate(
            [lax.dynamic_slice_in_dim(w, start, 512, 1) for w in (ffn_gate, ffn_lift, ffn_down.T)]
        )

    own, rest = quarter(place[0], p), opposite(quarter(1 - place[0], 1 - p))
    near, far = jnp.concatenate([own, twin(own)]), jnp.concatenate([rest, twin(rest)])

    swapped = moved(local, ("p",), lambda a: (1 - a,))
    mine = jnp.where(p == 0, local, swapped)
    across = moved(local, ("yh", "p"), lambda a, b: (1 - a, 0) if b == 0 else None)
    corner = moved(local, ("yh", "p"), lambda a, b: (1 - a, 1) if b == 0 else None)
    theirs = jnp.where(p == 0, across, corner)
    decoding = jnp.where(p == 0, swapped[:128], local[128:])
    gain_rows = jnp.broadcast_to(final_gain[None], (16, 512))
    tokens = around(jnp.concatenate([mine, theirs, decoding, gain_rows]), 256)
    gain = encoder_gain.reshape(4, 1, 512)
    query_gain = decoder_gain.reshape(4, 1, 512)
    early = swapped, across, corner
    chunks = gather_lines(near, far, (early, (place, gain, query_gain), tokens[1:4:2], tokens[2]))

    terms = ffn(place, tokens, gain, chunks)
    terms = lax.all_to_all(terms, ("yh", "p", "x"), 0, 0)
    query = query_rows(place, tokens, query_gain, query_weight)
    memory = memory_rows(place, terms, tokens)
    memory = [shifted(memory, k) for k in range(4)]
    *attended, columns = attention(
        place, lengths, query, memory, key_weight, value_weight, output_weight
    )
    summed = decoding.astype(f32)
    for k in range(4):
        summed = summed + shifted(attended[k], k).astype(f32)
    decoded = summed.astype(bf16)
    swapped = moved(jnp.where(p == 0, decoded, columns), ("p",), lambda a: (1 - a,))
    first = jnp.where(p == 0, columns, swapped)
    second = jnp.where(p == 0, swapped, decoded)
    return jnp.concatenate([first, second]).reshape(1, 2, 128, 512)


def solution(mesh):
    names = tuple(SIZES)
    fine = Mesh(mesh.devices.reshape(tuple(SIZES.values())), names)
    dp = ("yh", "z", "c")
    placed = (
        P("p", dp, None, "x"),
        P(dp),
        P(),
        P(dp, "x"),
        P(dp, "x"),
        P("x", dp),
        P("x"),
        P(),
        P(None, "x"),
        P(None, "x"),
        P(None, "x"),
        P("x", None),
    )
    return jax.shard_map(
        shards, mesh=fine, in_specs=placed, out_specs=P("p", dp, None, "x"), check_vma=False
    )
```

```python
import jax
import jax.numpy as jnp
import numpy as np
from jax import lax
from jax.experimental import pallas as pl
from jax.experimental.pallas import tpu as pltpu
from jax.sharding import Mesh, PartitionSpec as P

HEAD_DIM = 256
epsilon = 1e-06
SIZES = {"yh": 2, "z": 8, "c": 2, "p": 2, "x": 4}
PLANE = ("yh", "p", "x")
bf16, f32 = jnp.bfloat16, jnp.float32
MIB = 1 << 20


def moved(value, axes, route):
    dims = [SIZES[a] for a in axes]
    pairs = []
    for at in np.ndindex(*dims):
        to = route(*at)
        if to is not None:
            pairs.append((int(np.ravel_multi_index(at, dims)), int(np.ravel_multi_index(to, dims))))
    return lax.ppermute(value, axes, pairs)


def passed(value):
    return moved(
        value, ("z", "c"), lambda z, c: ((z + 1) % 8, c) if c == 0 else ((z - 1) % 8, c)
    )


def after(value, *others):
    if not others:
        return value

    def kernel(*refs):
        del refs

    return pl.pallas_call(
        kernel,
        in_specs=[anyplace()] * (1 + len(others)),
        out_specs=anyplace(),
        out_shape=jax.ShapeDtypeStruct(value.shape, value.dtype),
        input_output_aliases={0: 0},
        compiler_params=params(1),
    )(value, *others)


def gather_lines(near, far, ready):
    near, far = [near], [far]
    for k in range(3):
        near.append(after(passed(near[k]), *ready[k]))
        far.append(passed(far[k]))
    near.append(after(passed(near[3][:192]), *ready[3]))
    far.append(passed(far[3][:192]))
    return [v for line in (near, far) for v in line + [twin(chunk) for chunk in line[1:]]]


def opposite(value):
    return moved(value, ("yh", "p"), lambda a, b: (1 - a, 1 - b))


def shifted(value, k):
    return moved(value, ("x",), lambda a: ((a + k) % 4,)) if k else value


def around(value, cut):
    up, down = (lambda a: ((a + 1) % 4,)), (lambda a: ((a - 1) % 4,))
    first, third = moved(value, ("x",), up), moved(value, ("x",), down)
    second = moved(first[:cut], ("x",), up), moved(third[cut:], ("x",), down)
    return value, first, second, third


def twin(value):
    return moved(value, ("c",), lambda a: (1 - a,))


def whole(shape):
    return pl.BlockSpec(shape, lambda *_: (0,) * len(shape))


def params(mib=60):
    return pltpu.CompilerParams(vmem_limit_bytes=mib * MIB)


def smem():
    return pl.BlockSpec(memory_space=pltpu.SMEM)


def vmem():
    return pl.BlockSpec(memory_space=pltpu.VMEM)


def anyplace():
    return pl.BlockSpec(memory_space=pl.ANY)


CHUNKS = 9


def normed_block(block, scale, gain):
    return (block[...].astype(f32) * scale * gain.astype(f32)).astype(bf16)


def scale_of(blocks):
    square = 0.0
    for block in blocks:
        t = block[...].astype(f32)
        square = square + jnp.sum(t * t, axis=-1, keepdims=True)
    return lax.rsqrt(square * (1.0 / 2048) + epsilon)


def ffn_kernel(place, *refs):
    tokens, gain, refs = refs[:8], refs[8], refs[9:]
    chunks, (out, held, normed, sems) = refs[: 2 * CHUNKS], refs[2 * CHUNKS :]
    yh, x, z, c = place[0], place[2], place[3], place[4]
    first = pl.program_id(0) == 0
    ways = [(m, side) for side in range(2) for m in range(2)] + [(2, 0), (2, 1)]

    @pl.when(first)
    def _():
        for m, side in ways:
            for k in range(CHUNKS):
                chunk = chunks[side * CHUNKS + k]
                step, core = (k, c) if k < 5 else (k - 4, 1 - c)
                at = (z - step * (1 - 2 * core)) & 7
                for half in range(chunk.shape[0] // 192):
                    source = chunk.at[pl.ds(half * 192 + m * 64, 64)]
                    target = held.at[m, side, at, core ^ half]
                    pltpu.make_async_copy(source, target, sems.at[m, side]).start()

    def wait(*those):
        @pl.when(first)
        def _():
            for spot in those:
                pltpu.make_async_copy(held.at[spot], held.at[spot], sems.at[spot]).wait()

    for i in range(2):

        @pl.when(pl.program_id(0) == i)
        def _():
            blocks = tokens[i * 4 : (i + 1) * 4]
            scale = scale_of(blocks)
            for k, block in enumerate(blocks):
                b = (x - k) & 3
                normed[b] = normed_block(block, scale, gain[b])

    gate = lift = 0.0
    for side in range(2):
        b = (yh ^ side) * 2
        n = jnp.concatenate([normed[b], normed[b + 1]], 1)
        wait((0, side), (1, side))
        gate += jnp.dot(n, held[0, side].reshape(1024, 512), preferred_element_type=f32)
        lift += jnp.dot(n, held[1, side].reshape(1024, 512), preferred_element_type=f32)
    inner = 0.7978845608028654 * (gate + 0.044715 * (gate * gate * gate))
    hidden = (0.5 * gate * (1.0 + jnp.tanh(inner)) * lift).astype(bf16)
    wait((2, 0), (2, 1))
    for side in range(2):
        for k in range(2):
            rows = held[2, side, k * 4 : (k + 1) * 4].reshape(512, 512)
            part = lax.dot_general(
                hidden, rows, (((1,), (1,)), ((), ())), preferred_element_type=f32
            )
            out[:, (yh ^ side) * 2 + k] = part.astype(bf16).reshape(8, 32, 512)


def rows_at(rows, at):
    return pl.BlockSpec((rows, 512), lambda i, place: (at, 0))


def ffn(place, tokens, gain, chunks):
    first, second, (third, third_rest), fourth = tokens
    mine, theirs = (first, second, third, fourth), (first, second, third_rest, fourth)
    grid_spec = pltpu.PrefetchScalarGridSpec(
        num_scalar_prefetch=1,
        grid=(2,),
        in_specs=[rows_at(256, at) for at in (0, 0, 0, 0, 1, 1, 0, 1)]
        + [whole(gain.shape)]
        + [anyplace()] * len(chunks),
        out_specs=pl.BlockSpec((8, 4, 32, 512), lambda i, place: (place[0] ^ i, 0, 0, 0)),
        scratch_shapes=[
            pltpu.VMEM((3, 2, 8, 2, 64, 512), bf16),
            pltpu.VMEM((4, 256, 512), bf16),
            pltpu.SemaphoreType.DMA((3, 2)),
        ],
    )
    return pl.pallas_call(
        ffn_kernel,
        grid_spec=grid_spec,
        out_shape=jax.ShapeDtypeStruct((16, 4, 32, 512), bf16),
        compiler_params=params(),
        cost_estimate=pl.CostEstimate(
            flops=512 * 2048 * 512 * 6, bytes_accessed=10 * MIB, transcendentals=512 * 512
        ),
    )(place, *mine, *theirs, gain, *chunks)


def memory_kernel(place, terms, *refs):
    tokens, gains, out = refs[:4], refs[4:8], refs[8]
    square, kept = 0.0, []
    for i in range(4):
        b = (place[2] - i) & 3
        total = terms[0, b].astype(f32)
        for k in range(1, 16):
            total = total + terms[k, b].astype(f32)
        merged = tokens[i][...].astype(f32) + total
        square = square + jnp.sum(merged * merged, axis=-1, keepdims=True)
        kept.append(merged)
    scale = lax.rsqrt(square * (1.0 / 2048) + epsilon)
    for i in range(4):
        at = pl.ds(pl.multiple_of(((place[2] - i) & 3) * 512, 512), 512)
        rounded = (kept[i] * scale * gains[i][:1].astype(f32)).astype(bf16)
        out[:, at] = rounded


def memory_rows(place, terms, tokens):
    first, second, (third, third_rest), fourth = tokens
    grid_spec = pltpu.PrefetchScalarGridSpec(
        num_scalar_prefetch=1,
        grid=(1,),
        in_specs=[whole(terms.shape)]
        + [pl.BlockSpec((32, 512), lambda i, place: (place[1] * 4 + place[2], 0))] * 4
        + [rows_at(16, at) for at in (40, 40, 24, 40)],
        out_specs=whole((32, 2048)),
    )
    return pl.pallas_call(
        memory_kernel,
        grid_spec=grid_spec,
        out_shape=jax.ShapeDtypeStruct((32, 2048), bf16),
        compiler_params=params(16),
    )(place, terms, first, second, third, fourth, first, second, third_rest, fourth)


def query_kernel(place, t0, t1, t2, t3, gain, weight, wk, wv, wo, out, *held):
    kept, sems = held[:3], held[3]
    copies = [
        pltpu.make_async_copy(source, target, sems.at[i])
        for i, (source, target) in enumerate(zip((wk, wv, wo), kept))
    ]
    for copy in copies:
        copy.start()
    blocks = (t0, t1, t2, t3)
    scale = scale_of(blocks)
    total = 0.0
    for k, block in enumerate(blocks):
        b = (place[2] - k) & 3
        rows = weight[pl.ds(pl.multiple_of(b * 512, 512), 512), :]
        n = normed_block(block, scale, gain[b])
        total += jnp.dot(n, rows, preferred_element_type=f32)
    out[...] = total.astype(bf16)
    for copy in copies:
        copy.wait()


def query_rows(place, tokens, gain, weight, others):
    grid_spec = pltpu.PrefetchScalarGridSpec(
        num_scalar_prefetch=1,
        grid=(1,),
        in_specs=[rows_at(128, at) for at in (4, 4, 2, 4)]
        + [whole(gain.shape), whole(weight.shape)]
        + [anyplace()] * 3,
        out_specs=[whole((128, 512))] + [vmem()] * 3,
        scratch_shapes=[pltpu.SemaphoreType.DMA((3,))],
    )
    return pl.pallas_call(
        query_kernel,
        grid_spec=grid_spec,
        out_shape=[jax.ShapeDtypeStruct((128, 512), bf16)]
        + [jax.ShapeDtypeStruct(w.shape, bf16) for w in others],
        compiler_params=params(40),
        cost_estimate=pl.CostEstimate(
            flops=2 * 128 * 2048 * 512, bytes_accessed=10 * MIB, transcendentals=0
        ),
    )(place, tokens[0], tokens[1], tokens[2][1], tokens[3], gain, weight, *others)


def attention_kernel(place, lengths, query, m0, m1, m2, m3, wk, wv, wo, *refs):
    outs, columns = refs[:4], refs[4]
    x = place[2]
    blocks = (m0, m1, m2, m3)
    mine = pl.ds(pl.multiple_of(x * 512, 512), 512)
    for k, block in enumerate(blocks):
        columns[pl.ds(pl.multiple_of(((x - k) & 3) * 32, 32), 32), :] = block[:, mine]
    memory = jnp.concatenate([block[...] for block in blocks], 0)
    keys, values = (
        jnp.dot(memory, w[...], preferred_element_type=f32).astype(bf16) for w in (wk, wv)
    )
    spots = lax.broadcasted_iota(jnp.int32, (128, 128), 1)
    positions = (((x - (spots >> 5)) & 3) << 5) + (spots & 31)
    valid = positions < lengths[place[1]]
    contexts = []
    for h in range(2):
        at = slice(h * HEAD_DIM, (h + 1) * HEAD_DIM)
        scores = lax.dot_general(
            query[:, at], keys[:, at], (((1,), (1,)), ((), ())), preferred_element_type=f32
        )
        scores = jnp.where(valid, scores, -1e30)
        weights = jnp.exp(scores - jnp.max(scores, axis=-1, keepdims=True))
        probs = (weights / jnp.sum(weights, axis=-1, keepdims=True)).astype(bf16)
        contexts.append(jnp.dot(probs, values[:, at], preferred_element_type=f32).astype(bf16))
    context = jnp.concatenate(contexts, axis=1)
    for k in range(4):
        at = pl.ds(pl.multiple_of(((x + k) & 3) * 512, 512), 512)
        part = jnp.dot(context, wo[:, at], preferred_element_type=f32)
        outs[k][...] = part.astype(bf16)


def attention(place, lengths, query, memory, wk, wv, wo):
    return pl.pallas_call(
        attention_kernel,
        in_specs=[smem()] * 2 + [vmem()] * 8,
        out_specs=[vmem()] * 5,
        out_shape=[jax.ShapeDtypeStruct((128, 512), bf16)] * 5,
        compiler_params=params(16),
        cost_estimate=pl.CostEstimate(
            flops=6 * 128 * 2048 * 512, bytes_accessed=8 * MIB, transcendentals=128 * 256
        ),
    )(place, lengths, query, *memory, wk, wv, wo)


def shards(
    streams,
    lengths,
    encoder_gain,
    ffn_gate,
    ffn_lift,
    ffn_down,
    final_gain,
    decoder_gain,
    query_weight,
    key_weight,
    value_weight,
    output_weight,
):
    place = jnp.stack([lax.axis_index(a) for a in ("yh", "p", "x", "z", "c")]).astype(jnp.int32)
    p, x = place[1], place[2]
    local = streams[0].reshape(256, 512)

    def quarter(yh, p):
        start = (p * 2 + yh) * 512
        return jnp.concatenate(
            [lax.dynamic_slice_in_dim(w, start, 512, 1) for w in (ffn_gate, ffn_lift, ffn_down.T)]
        )

    own, rest = quarter(place[0], p), opposite(quarter(1 - place[0], 1 - p))
    near, far = jnp.concatenate([own, twin(own)]), jnp.concatenate([rest, twin(rest)])

    swapped = moved(local, ("p",), lambda a: (1 - a,))
    mine = jnp.where(p == 0, local, swapped)
    across = moved(local, ("yh", "p"), lambda a, b: (1 - a, 0) if b == 0 else None)
    corner = moved(local, ("yh", "p"), lambda a, b: (1 - a, 1) if b == 0 else None)
    theirs = jnp.where(p == 0, across, corner)
    decoding = jnp.where(p == 0, swapped[:128], local[128:])
    gain_rows = jnp.broadcast_to(final_gain[None], (16, 512))
    tokens = around(jnp.concatenate([mine, theirs, decoding, gain_rows]), 256)
    gain = encoder_gain.reshape(4, 1, 512)
    query_gain = decoder_gain.reshape(4, 1, 512)
    early = swapped, across, corner
    chunks = gather_lines(near, far, (early, (place, gain, query_gain), tokens[1:4:2], tokens[2]))

    terms = ffn(place, tokens, gain, chunks)
    terms = lax.all_to_all(terms, ("yh", "p", "x"), 0, 0)
    query, *others = query_rows(
        place, tokens, query_gain, query_weight, (key_weight, value_weight, output_weight)
    )
    memory = memory_rows(place, terms, tokens)
    memory = [shifted(memory, k) for k in range(4)]
    *attended, columns = attention(place, lengths, query, memory, *others)
    summed = decoding.astype(f32)
    for k in range(4):
        summed = summed + shifted(attended[k], k).astype(f32)
    decoded = summed.astype(bf16)
    swapped = moved(jnp.where(p == 0, decoded, columns), ("p",), lambda a: (1 - a,))
    first = jnp.where(p == 0, columns, swapped)
    second = jnp.where(p == 0, swapped, decoded)
    return jnp.concatenate([first, second]).reshape(1, 2, 128, 512)


def solution(mesh):
    names = tuple(SIZES)
    fine = Mesh(mesh.devices.reshape(tuple(SIZES.values())), names)
    dp = ("yh", "z", "c")
    placed = (
        P("p", dp, None, "x"),
        P(dp),
        P(),
        P(dp, "x"),
        P(dp, "x"),
        P("x", dp),
        P("x"),
        P(),
        P(None, "x"),
        P(None, "x"),
        P(None, "x"),
        P("x", None),
    )
    return jax.shard_map(
        shards, mesh=fine, in_specs=placed, out_specs=P("p", dp, None, "x"), check_vma=False
    )
```

```python
import jax
import jax.numpy as jnp
import numpy as np
from jax import lax
from jax.experimental import pallas as pl
from jax.experimental.pallas import tpu as pltpu
from jax.sharding import Mesh, PartitionSpec as P

HEAD_DIM = 256
epsilon = 1e-06
SIZES = {"yh": 2, "z": 8, "c": 2, "p": 2, "x": 4}
PLANE = ("yh", "p", "x")
bf16, f32 = jnp.bfloat16, jnp.float32
MIB = 1 << 20


def moved(value, axes, route):
    dims = [SIZES[a] for a in axes]
    pairs = []
    for at in np.ndindex(*dims):
        to = route(*at)
        if to is not None:
            pairs.append((int(np.ravel_multi_index(at, dims)), int(np.ravel_multi_index(to, dims))))
    return lax.ppermute(value, axes, pairs)


def passed(value):
    return moved(
        value, ("z", "c"), lambda z, c: ((z + 1) % 8, c) if c == 0 else ((z - 1) % 8, c)
    )


def after(value, *others):
    if not others:
        return value

    def kernel(*refs):
        del refs

    return pl.pallas_call(
        kernel,
        in_specs=[anyplace()] * (1 + len(others)),
        out_specs=anyplace(),
        out_shape=jax.ShapeDtypeStruct(value.shape, value.dtype),
        input_output_aliases={0: 0},
        compiler_params=params(1),
    )(value, *others)


def gather_lines(near, far, ready):
    near, far = [near], [far]
    for k in range(3):
        near.append(after(passed(near[k]), *ready[k]))
        far.append(passed(far[k]))
    near.append(after(passed(near[3][:192]), *ready[3]))
    far.append(passed(far[3][:192]))
    return [v for line in (near, far) for v in line + [twin(chunk) for chunk in line[1:]]]


def opposite(value):
    return moved(value, ("yh", "p"), lambda a, b: (1 - a, 1 - b))


def shifted(value, k):
    return moved(value, ("x",), lambda a: ((a + k) % 4,)) if k else value


def around(value, cut):
    up, down = (lambda a: ((a + 1) % 4,)), (lambda a: ((a - 1) % 4,))
    first, third = moved(value, ("x",), up), moved(value, ("x",), down)
    second = moved(first[:cut], ("x",), up), moved(third[cut:], ("x",), down)
    return value, first, second, third


def twin(value):
    return moved(value, ("c",), lambda a: (1 - a,))


def whole(shape):
    return pl.BlockSpec(shape, lambda *_: (0,) * len(shape))


def params(mib=60):
    return pltpu.CompilerParams(vmem_limit_bytes=mib * MIB)


def smem():
    return pl.BlockSpec(memory_space=pltpu.SMEM)


def vmem():
    return pl.BlockSpec(memory_space=pltpu.VMEM)


def anyplace():
    return pl.BlockSpec(memory_space=pl.ANY)


CHUNKS = 9


def normed_block(block, scale, gain):
    return (block[...].astype(f32) * scale * gain.astype(f32)).astype(bf16)


def scale_of(blocks):
    square = 0.0
    for block in blocks:
        t = block[...].astype(f32)
        square = square + jnp.sum(t * t, axis=-1, keepdims=True)
    return lax.rsqrt(square * (1.0 / 2048) + epsilon)


def halves_of(chunk, core, part):
    return [
        chunk[pl.ds(pl.multiple_of((a ^ core) * 192 + part * 64, 64), 64), :] for a in range(2)
    ]


def whole_chunks(place, chunks):
    yh, z, c = place[0], place[3], place[4]
    found = []
    for side in range(2):
        for k in (0, 1, 2, 3, 5, 6, 7):
            step, core = (k, c) if k < 5 else (k - 4, 1 - c)
            at = (yh ^ side) * 8 + ((z - step * (1 - 2 * core)) & 7)
            found.append((at, chunks[side * CHUNKS + k], core))
    return found


def first_kernel(place, *refs):
    tokens, gain, given = refs[:8], refs[8], refs[9:23]
    gate, lift, last, normed = refs[23:]
    yh, x, z = place[0], place[2], place[3]
    for i in range(2):
        rows = slice(i * 256, (i + 1) * 256)
        blocks = tokens[i * 4 : (i + 1) * 4]
        scale = scale_of(blocks)
        for k, block in enumerate(blocks):
            b = (x - k) & 3
            value = normed_block(block, scale, gain[b])
            for j in range(4):
                normed[b * 4 + j, rows] = value[:, j * 128 : (j + 1) * 128]
    chunks = [None] * (2 * CHUNKS)
    for j, chunk in enumerate(given):
        chunks[j // 7 * CHUNKS + (0, 1, 2, 3, 5, 6, 7)[j % 7]] = chunk
    spots = whole_chunks(place, chunks)
    for part, out in enumerate((gate, lift)):
        w = jnp.concatenate(
            [half for _, chunk, core in spots for half in halves_of(chunk, core, part)], 0
        )
        for i in range(2):
            rows = slice(i * 256, (i + 1) * 256)
            n = jnp.concatenate([normed[at, rows] for at, _, _ in spots], 1)
            out[rows] = jnp.dot(n, w, preferred_element_type=f32)
    for side in range(2):
        last[side] = normed[(yh ^ side) * 8 + ((z + 4) & 7)]


def second_kernel(place, gate, lift, last, *refs):
    chunks, out = refs[: 2 * CHUNKS], refs[2 * CHUNKS]
    yh, z, c = place[0], place[3], place[4]

    def rest_of(part):
        rows = slice(part * 64, (part + 1) * 64)
        found = []
        for side in range(2):
            own, twin = (chunks[side * CHUNKS + k][rows] for k in (4, 8))
            found += [jnp.where(c == 0, own, twin), jnp.where(c == 0, twin, own)]
        return jnp.concatenate(found, 0)

    n = jnp.concatenate([last[0], last[1]], 1)
    g = gate[...] + jnp.dot(n, rest_of(0), preferred_element_type=f32)
    up = lift[...] + jnp.dot(n, rest_of(1), preferred_element_type=f32)
    inner = 0.7978845608028654 * (g + 0.044715 * (g * g * g))
    hidden = (0.5 * g * (1.0 + jnp.tanh(inner)) * up).astype(bf16)
    spots = whole_chunks(place, chunks)
    pairs = [
        (
            [spots[k][0], spots[k + 1][0]],
            jnp.concatenate(halves_of(*spots[k][1:], 2) + halves_of(*spots[k + 1][1:], 2), 0),
        )
        for k in range(0, 14, 2)
    ]
    pairs.append(([(yh ^ side) * 8 + ((z + 4) & 7) for side in range(2)], rest_of(2)))
    for places, w in pairs:
        sums = lax.dot_general(hidden, w, (((1,), (1,)), ((), ())), preferred_element_type=f32)
        sums = sums.astype(bf16)
        for j, at in enumerate(places):
            lanes = pl.ds(pl.multiple_of((at & 3) * 128, 128), 128)
            out[:, at >> 2, :, lanes] = sums[:, j * 128 : (j + 1) * 128].reshape(8, 32, 128)


def rows_at(rows, at):
    return pl.BlockSpec((rows, 512), lambda i, place: (at, 0))


def ffn(place, tokens, gain, chunks):
    first, second, (third, third_rest), fourth = tokens
    mine, theirs = (first, second, third, fourth), (first, second, third_rest, fourth)
    given = [chunk for chunk in chunks if chunk.shape[0] == 384]
    grid_spec = pltpu.PrefetchScalarGridSpec(
        num_scalar_prefetch=1,
        grid=(1,),
        in_specs=[rows_at(256, at) for at in (0, 0, 0, 0, 1, 1, 0, 1)]
        + [whole(gain.shape)]
        + [vmem()] * len(given),
        out_specs=[vmem()] * 3,
        scratch_shapes=[pltpu.VMEM((16, 512, 128), bf16)],
    )
    gate, lift, last = pl.pallas_call(
        first_kernel,
        grid_spec=grid_spec,
        out_shape=[jax.ShapeDtypeStruct((512, 512), f32)] * 2
        + [jax.ShapeDtypeStruct((2, 512, 128), bf16)],
        compiler_params=params(24),
        cost_estimate=pl.CostEstimate(
            flops=512 * 1792 * 512 * 4, bytes_accessed=4 * MIB, transcendentals=0
        ),
    )(place, *mine, *theirs, gain, *given)
    grid_spec = pltpu.PrefetchScalarGridSpec(
        num_scalar_prefetch=1,
        grid=(2,),
        in_specs=[pl.BlockSpec((256, 512), lambda i, place: (i, 0))] * 2
        + [pl.BlockSpec((2, 256, 128), lambda i, place: (0, i, 0))]
        + [vmem()] * len(chunks),
        out_specs=pl.BlockSpec((8, 4, 32, 512), lambda i, place: (place[0] ^ i, 0, 0, 0)),
    )
    return pl.pallas_call(
        second_kernel,
        grid_spec=grid_spec,
        out_shape=jax.ShapeDtypeStruct((16, 4, 32, 512), bf16),
        compiler_params=params(24),
        cost_estimate=pl.CostEstimate(
            flops=512 * 2304 * 512 * 2, bytes_accessed=4 * MIB, transcendentals=512 * 512
        ),
    )(place, gate, lift, last, *chunks)


def memory_kernel(place, terms, *refs):
    tokens, gains, out = refs[:4], refs[4:8], refs[8]
    square, kept = 0.0, []
    for i in range(4):
        b = (place[2] - i) & 3
        total = terms[0, b].astype(f32)
        for k in range(1, 16):
            total = total + terms[k, b].astype(f32)
        merged = tokens[i][...].astype(f32) + total
        square = square + jnp.sum(merged * merged, axis=-1, keepdims=True)
        kept.append(merged)
    scale = lax.rsqrt(square * (1.0 / 2048) + epsilon)
    for i in range(4):
        at = pl.ds(pl.multiple_of(((place[2] - i) & 3) * 512, 512), 512)
        rounded = (kept[i] * scale * gains[i][:1].astype(f32)).astype(bf16)
        out[:, at] = rounded


def memory_rows(place, terms, tokens):
    first, second, (third, third_rest), fourth = tokens
    grid_spec = pltpu.PrefetchScalarGridSpec(
        num_scalar_prefetch=1,
        grid=(1,),
        in_specs=[whole(terms.shape)]
        + [pl.BlockSpec((32, 512), lambda i, place: (place[1] * 4 + place[2], 0))] * 4
        + [rows_at(16, at) for at in (40, 40, 24, 40)],
        out_specs=whole((32, 2048)),
    )
    return pl.pallas_call(
        memory_kernel,
        grid_spec=grid_spec,
        out_shape=jax.ShapeDtypeStruct((32, 2048), bf16),
        compiler_params=params(16),
    )(place, terms, first, second, third, fourth, first, second, third_rest, fourth)


def query_kernel(place, t0, t1, t2, t3, gain, weight, wk, wv, wo, out, *held):
    kept, sems = held[:3], held[3]
    copies = [
        pltpu.make_async_copy(source, target, sems.at[i])
        for i, (source, target) in enumerate(zip((wk, wv, wo), kept))
    ]
    for copy in copies:
        copy.start()
    blocks = (t0, t1, t2, t3)
    scale = scale_of(blocks)
    total = 0.0
    for k, block in enumerate(blocks):
        b = (place[2] - k) & 3
        rows = weight[pl.ds(pl.multiple_of(b * 512, 512), 512), :]
        n = normed_block(block, scale, gain[b])
        total += jnp.dot(n, rows, preferred_element_type=f32)
    out[...] = total.astype(bf16)
    for copy in copies:
        copy.wait()


def query_rows(place, tokens, gain, weight, others):
    grid_spec = pltpu.PrefetchScalarGridSpec(
        num_scalar_prefetch=1,
        grid=(1,),
        in_specs=[rows_at(128, at) for at in (4, 4, 2, 4)]
        + [whole(gain.shape), whole(weight.shape)]
        + [anyplace()] * 3,
        out_specs=[whole((128, 512))] + [vmem()] * 3,
        scratch_shapes=[pltpu.SemaphoreType.DMA((3,))],
    )
    return pl.pallas_call(
        query_kernel,
        grid_spec=grid_spec,
        out_shape=[jax.ShapeDtypeStruct((128, 512), bf16)]
        + [jax.ShapeDtypeStruct(w.shape, bf16) for w in others],
        compiler_params=params(40),
        cost_estimate=pl.CostEstimate(
            flops=2 * 128 * 2048 * 512, bytes_accessed=10 * MIB, transcendentals=0
        ),
    )(place, tokens[0], tokens[1], tokens[2][1], tokens[3], gain, weight, *others)


def attention_kernel(place, lengths, query, m0, m1, m2, m3, wk, wv, wo, *refs):
    outs, columns = refs[:4], refs[4]
    x = place[2]
    blocks = (m0, m1, m2, m3)
    mine = pl.ds(pl.multiple_of(x * 512, 512), 512)
    for k, block in enumerate(blocks):
        columns[pl.ds(pl.multiple_of(((x - k) & 3) * 32, 32), 32), :] = block[:, mine]
    memory = jnp.concatenate([block[...] for block in blocks], 0)
    keys, values = (
        jnp.dot(memory, w[...], preferred_element_type=f32).astype(bf16) for w in (wk, wv)
    )
    spots = lax.broadcasted_iota(jnp.int32, (128, 128), 1)
    positions = (((x - (spots >> 5)) & 3) << 5) + (spots & 31)
    valid = positions < lengths[place[1]]
    contexts = []
    for h in range(2):
        at = slice(h * HEAD_DIM, (h + 1) * HEAD_DIM)
        scores = lax.dot_general(
            query[:, at], keys[:, at], (((1,), (1,)), ((), ())), preferred_element_type=f32
        )
        scores = jnp.where(valid, scores, -1e30)
        weights = jnp.exp(scores - jnp.max(scores, axis=-1, keepdims=True))
        probs = (weights / jnp.sum(weights, axis=-1, keepdims=True)).astype(bf16)
        contexts.append(jnp.dot(probs, values[:, at], preferred_element_type=f32).astype(bf16))
    context = jnp.concatenate(contexts, axis=1)
    for k in range(4):
        at = pl.ds(pl.multiple_of(((x + k) & 3) * 512, 512), 512)
        part = jnp.dot(context, wo[:, at], preferred_element_type=f32)
        outs[k][...] = part.astype(bf16)


def attention(place, lengths, query, memory, wk, wv, wo):
    return pl.pallas_call(
        attention_kernel,
        in_specs=[smem()] * 2 + [vmem()] * 8,
        out_specs=[vmem()] * 5,
        out_shape=[jax.ShapeDtypeStruct((128, 512), bf16)] * 5,
        compiler_params=params(16),
        cost_estimate=pl.CostEstimate(
            flops=6 * 128 * 2048 * 512, bytes_accessed=8 * MIB, transcendentals=128 * 256
        ),
    )(place, lengths, query, *memory, wk, wv, wo)


def shards(
    streams,
    lengths,
    encoder_gain,
    ffn_gate,
    ffn_lift,
    ffn_down,
    final_gain,
    decoder_gain,
    query_weight,
    key_weight,
    value_weight,
    output_weight,
):
    place = jnp.stack([lax.axis_index(a) for a in ("yh", "p", "x", "z", "c")]).astype(jnp.int32)
    p, x = place[1], place[2]
    local = streams[0].reshape(256, 512)

    def quarter(yh, p):
        start = (p * 2 + yh) * 512
        return jnp.concatenate(
            [lax.dynamic_slice_in_dim(w, start, 512, 1) for w in (ffn_gate, ffn_lift, ffn_down.T)]
        )

    own, rest = quarter(place[0], p), opposite(quarter(1 - place[0], 1 - p))
    near, far = jnp.concatenate([own, twin(own)]), jnp.concatenate([rest, twin(rest)])

    swapped = moved(local, ("p",), lambda a: (1 - a,))
    mine = jnp.where(p == 0, local, swapped)
    across = moved(local, ("yh", "p"), lambda a, b: (1 - a, 0) if b == 0 else None)
    corner = moved(local, ("yh", "p"), lambda a, b: (1 - a, 1) if b == 0 else None)
    theirs = jnp.where(p == 0, across, corner)
    decoding = jnp.where(p == 0, swapped[:128], local[128:])
    gain_rows = jnp.broadcast_to(final_gain[None], (16, 512))
    tokens = around(jnp.concatenate([mine, theirs, decoding, gain_rows]), 256)
    gain = encoder_gain.reshape(4, 1, 512)
    query_gain = decoder_gain.reshape(4, 1, 512)
    early = swapped, across, corner
    chunks = gather_lines(near, far, (early, (place, gain, query_gain), tokens[1:4:2], tokens[2]))

    terms = ffn(place, tokens, gain, chunks)
    terms = lax.all_to_all(terms, ("yh", "p", "x"), 0, 0)
    query, *others = query_rows(
        place, tokens, query_gain, query_weight, (key_weight, value_weight, output_weight)
    )
    memory = memory_rows(place, terms, tokens)
    memory = [shifted(memory, k) for k in range(4)]
    *attended, columns = attention(place, lengths, query, memory, *others)
    summed = decoding.astype(f32)
    for k in range(4):
        summed = summed + shifted(attended[k], k).astype(f32)
    decoded = summed.astype(bf16)
    swapped = moved(jnp.where(p == 0, decoded, columns), ("p",), lambda a: (1 - a,))
    first = jnp.where(p == 0, columns, swapped)
    second = jnp.where(p == 0, swapped, decoded)
    return jnp.concatenate([first, second]).reshape(1, 2, 128, 512)


def solution(mesh):
    names = tuple(SIZES)
    fine = Mesh(mesh.devices.reshape(tuple(SIZES.values())), names)
    dp = ("yh", "z", "c")
    placed = (
        P("p", dp, None, "x"),
        P(dp),
        P(),
        P(dp, "x"),
        P(dp, "x"),
        P("x", dp),
        P("x"),
        P(),
        P(None, "x"),
        P(None, "x"),
        P(None, "x"),
        P("x", None),
    )
    return jax.shard_map(
        shards, mesh=fine, in_specs=placed, out_specs=P("p", dp, None, "x"), check_vma=False
    )
```

```python
import jax
import jax.numpy as jnp
import numpy as np
from jax import lax
from jax.experimental import pallas as pl
from jax.experimental.pallas import tpu as pltpu
from jax.sharding import Mesh, PartitionSpec as P

HEAD_DIM = 256
epsilon = 1e-06
SIZES = {"yh": 2, "z": 8, "c": 2, "p": 2, "x": 4}
PLANE = ("yh", "p", "x")
bf16, f32 = jnp.bfloat16, jnp.float32
MIB = 1 << 20


def moved(value, axes, route):
    dims = [SIZES[a] for a in axes]
    pairs = []
    for at in np.ndindex(*dims):
        to = route(*at)
        if to is not None:
            pairs.append((int(np.ravel_multi_index(at, dims)), int(np.ravel_multi_index(to, dims))))
    return lax.ppermute(value, axes, pairs)


def passed(value):
    return moved(
        value, ("z", "c"), lambda z, c: ((z + 1) % 8, c) if c == 0 else ((z - 1) % 8, c)
    )


def after(value, *others):
    if not others:
        return value

    def kernel(*refs):
        del refs

    return pl.pallas_call(
        kernel,
        in_specs=[anyplace()] * (1 + len(others)),
        out_specs=anyplace(),
        out_shape=jax.ShapeDtypeStruct(value.shape, value.dtype),
        input_output_aliases={0: 0},
        compiler_params=params(1),
    )(value, *others)


def gather_lines(near, far, ready):
    near, far = [near], [far]
    for k in range(3):
        near.append(after(passed(near[k]), *ready[k]))
        far.append(passed(far[k]))
    near.append(passed(near[3][:192]))
    far.append(passed(far[3][:192]))
    return [v for line in (near, far) for v in line + [twin(chunk) for chunk in line[1:4]]]


def opposite(value):
    return moved(value, ("yh", "p"), lambda a, b: (1 - a, 1 - b))


def shifted(value, k):
    return moved(value, ("x",), lambda a: ((a + k) % 4,)) if k else value


def around(value, cut):
    up, down = (lambda a: ((a + 1) % 4,)), (lambda a: ((a - 1) % 4,))
    first, third = moved(value, ("x",), up), moved(value, ("x",), down)
    second = moved(first[:cut], ("x",), up), moved(third[cut:], ("x",), down)
    return value, first, second, third


def twin(value):
    return moved(value, ("c",), lambda a: (1 - a,))


def whole(shape):
    return pl.BlockSpec(shape, lambda *_: (0,) * len(shape))


def params(mib=60):
    return pltpu.CompilerParams(vmem_limit_bytes=mib * MIB)


def smem():
    return pl.BlockSpec(memory_space=pltpu.SMEM)


def vmem():
    return pl.BlockSpec(memory_space=pltpu.VMEM)


def anyplace():
    return pl.BlockSpec(memory_space=pl.ANY)


CHUNKS = 9


def normed_block(block, scale, gain):
    return (block[...].astype(f32) * scale * gain.astype(f32)).astype(bf16)


def scale_of(blocks):
    square = 0.0
    for block in blocks:
        t = block[...].astype(f32)
        square = square + jnp.sum(t * t, axis=-1, keepdims=True)
    return lax.rsqrt(square * (1.0 / 2048) + epsilon)


def halves_of(chunk, core, part):
    return [
        chunk[pl.ds(pl.multiple_of((a ^ core) * 192 + part * 64, 64), 64), :] for a in range(2)
    ]


def whole_chunks(place, chunks):
    yh, z, c = place[0], place[3], place[4]
    found = []
    for side in range(2):
        for k in (0, 1, 2, 3, 5, 6, 7):
            step, core = (k, c) if k < 5 else (k - 4, 1 - c)
            at = (yh ^ side) * 8 + ((z - step * (1 - 2 * core)) & 7)
            found.append((at, chunks[side * CHUNKS + k], core))
    return found


def first_kernel(place, *refs):
    tokens, gain, given = refs[:8], refs[8], refs[9:23]
    gate, lift, last, normed = refs[23:]
    yh, x, z = place[0], place[2], place[3]
    for i in range(2):
        rows = slice(i * 256, (i + 1) * 256)
        blocks = tokens[i * 4 : (i + 1) * 4]
        scale = scale_of(blocks)
        for k, block in enumerate(blocks):
            b = (x - k) & 3
            value = normed_block(block, scale, gain[b])
            for j in range(4):
                normed[b * 4 + j, rows] = value[:, j * 128 : (j + 1) * 128]
    chunks = [None] * (2 * CHUNKS)
    for j, chunk in enumerate(given):
        chunks[j // 7 * CHUNKS + (0, 1, 2, 3, 5, 6, 7)[j % 7]] = chunk
    spots = whole_chunks(place, chunks)
    for part, out in enumerate((gate, lift)):
        w = jnp.concatenate(
            [half for _, chunk, core in spots for half in halves_of(chunk, core, part)], 0
        )
        for i in range(2):
            rows = slice(i * 256, (i + 1) * 256)
            n = jnp.concatenate([normed[at, rows] for at, _, _ in spots], 1)
            out[rows] = jnp.dot(n, w, preferred_element_type=f32)
    for side in range(2):
        last[side] = normed[(yh ^ side) * 8 + ((z + 4) & 7)]


def second_kernel(place, gate, lift, last, *refs):
    chunks, out = refs[: 2 * CHUNKS], refs[2 * CHUNKS]
    yh, z, c = place[0], place[3], place[4]

    def rest_of(part):
        rows = slice(part * 64, (part + 1) * 64)
        found = []
        for side in range(2):
            own, twin = (chunks[side * CHUNKS + k][rows] for k in (4, 8))
            found += [jnp.where(c == 0, own, twin), jnp.where(c == 0, twin, own)]
        return jnp.concatenate(found, 0)

    n = jnp.concatenate([last[0], last[1]], 1)
    g = gate[...] + jnp.dot(n, rest_of(0), preferred_element_type=f32)
    up = lift[...] + jnp.dot(n, rest_of(1), preferred_element_type=f32)
    inner = 0.7978845608028654 * (g + 0.044715 * (g * g * g))
    hidden = (0.5 * g * (1.0 + jnp.tanh(inner)) * up).astype(bf16)
    spots = whole_chunks(place, chunks)
    pairs = [
        (
            [spots[k][0], spots[k + 1][0]],
            jnp.concatenate(halves_of(*spots[k][1:], 2) + halves_of(*spots[k + 1][1:], 2), 0),
        )
        for k in range(0, 14, 2)
    ]
    pairs.append(([(yh ^ side) * 8 + ((z + 4) & 7) for side in range(2)], rest_of(2)))
    for places, w in pairs:
        sums = lax.dot_general(hidden, w, (((1,), (1,)), ((), ())), preferred_element_type=f32)
        sums = sums.astype(bf16)
        for j, at in enumerate(places):
            lanes = pl.ds(pl.multiple_of((at & 3) * 128, 128), 128)
            out[:, at >> 2, :, lanes] = sums[:, j * 128 : (j + 1) * 128].reshape(8, 32, 128)


def rows_at(rows, at):
    return pl.BlockSpec((rows, 512), lambda i, place: (at, 0))


def ffn(place, tokens, gain, chunks):
    first, second, (third, third_rest), fourth = tokens
    mine, theirs = (first, second, third, fourth), (first, second, third_rest, fourth)
    given = [chunk for chunk in chunks if chunk.shape[0] == 384]
    grid_spec = pltpu.PrefetchScalarGridSpec(
        num_scalar_prefetch=1,
        grid=(1,),
        in_specs=[rows_at(256, at) for at in (0, 0, 0, 0, 1, 1, 0, 1)]
        + [whole(gain.shape)]
        + [vmem()] * len(given),
        out_specs=[vmem()] * 3,
        scratch_shapes=[pltpu.VMEM((16, 512, 128), bf16)],
    )
    gate, lift, last = pl.pallas_call(
        first_kernel,
        grid_spec=grid_spec,
        out_shape=[jax.ShapeDtypeStruct((512, 512), f32)] * 2
        + [jax.ShapeDtypeStruct((2, 512, 128), bf16)],
        compiler_params=params(24),
        cost_estimate=pl.CostEstimate(
            flops=512 * 1792 * 512 * 4, bytes_accessed=4 * MIB, transcendentals=0
        ),
    )(place, *mine, *theirs, gain, *given)
    lines = []
    for line in (chunks[: CHUNKS - 1], chunks[CHUNKS - 1 :]):
        arrived = after(line[4], last)
        lines += line[:4] + [arrived] + line[5:] + [twin(arrived)]
    chunks = lines
    grid_spec = pltpu.PrefetchScalarGridSpec(
        num_scalar_prefetch=1,
        grid=(2,),
        in_specs=[pl.BlockSpec((256, 512), lambda i, place: (i, 0))] * 2
        + [pl.BlockSpec((2, 256, 128), lambda i, place: (0, i, 0))]
        + [vmem()] * len(chunks),
        out_specs=pl.BlockSpec((8, 4, 32, 512), lambda i, place: (place[0] ^ i, 0, 0, 0)),
    )
    return pl.pallas_call(
        second_kernel,
        grid_spec=grid_spec,
        out_shape=jax.ShapeDtypeStruct((16, 4, 32, 512), bf16),
        compiler_params=params(24),
        cost_estimate=pl.CostEstimate(
            flops=512 * 2304 * 512 * 2, bytes_accessed=4 * MIB, transcendentals=512 * 512
        ),
    )(place, gate, lift, last, *chunks)


def memory_kernel(place, terms, *refs):
    tokens, gains, out = refs[:4], refs[4:8], refs[8]
    square, kept = 0.0, []
    for i in range(4):
        b = (place[2] - i) & 3
        total = terms[0, b].astype(f32)
        for k in range(1, 16):
            total = total + terms[k, b].astype(f32)
        merged = tokens[i][...].astype(f32) + total
        square = square + jnp.sum(merged * merged, axis=-1, keepdims=True)
        kept.append(merged)
    scale = lax.rsqrt(square * (1.0 / 2048) + epsilon)
    for i in range(4):
        at = pl.ds(pl.multiple_of(((place[2] - i) & 3) * 512, 512), 512)
        rounded = (kept[i] * scale * gains[i][:1].astype(f32)).astype(bf16)
        out[:, at] = rounded


def memory_rows(place, terms, tokens):
    first, second, (third, third_rest), fourth = tokens
    grid_spec = pltpu.PrefetchScalarGridSpec(
        num_scalar_prefetch=1,
        grid=(1,),
        in_specs=[whole(terms.shape)]
        + [pl.BlockSpec((32, 512), lambda i, place: (place[1] * 4 + place[2], 0))] * 4
        + [rows_at(16, at) for at in (40, 40, 24, 40)],
        out_specs=whole((32, 2048)),
    )
    return pl.pallas_call(
        memory_kernel,
        grid_spec=grid_spec,
        out_shape=jax.ShapeDtypeStruct((32, 2048), bf16),
        compiler_params=params(16),
    )(place, terms, first, second, third, fourth, first, second, third_rest, fourth)


def query_kernel(place, t0, t1, t2, t3, gain, weight, wk, wv, wo, out, *held):
    kept, sems = held[:3], held[3]
    copies = [
        pltpu.make_async_copy(source, target, sems.at[i])
        for i, (source, target) in enumerate(zip((wk, wv, wo), kept))
    ]
    for copy in copies:
        copy.start()
    blocks = (t0, t1, t2, t3)
    scale = scale_of(blocks)
    total = 0.0
    for k, block in enumerate(blocks):
        b = (place[2] - k) & 3
        rows = weight[pl.ds(pl.multiple_of(b * 512, 512), 512), :]
        n = normed_block(block, scale, gain[b])
        total += jnp.dot(n, rows, preferred_element_type=f32)
    out[...] = total.astype(bf16)
    for copy in copies:
        copy.wait()


def query_rows(place, tokens, gain, weight, others):
    grid_spec = pltpu.PrefetchScalarGridSpec(
        num_scalar_prefetch=1,
        grid=(1,),
        in_specs=[rows_at(128, at) for at in (4, 4, 2, 4)]
        + [whole(gain.shape), whole(weight.shape)]
        + [anyplace()] * 3,
        out_specs=[whole((128, 512))] + [vmem()] * 3,
        scratch_shapes=[pltpu.SemaphoreType.DMA((3,))],
    )
    return pl.pallas_call(
        query_kernel,
        grid_spec=grid_spec,
        out_shape=[jax.ShapeDtypeStruct((128, 512), bf16)]
        + [jax.ShapeDtypeStruct(w.shape, bf16) for w in others],
        compiler_params=params(40),
        cost_estimate=pl.CostEstimate(
            flops=2 * 128 * 2048 * 512, bytes_accessed=10 * MIB, transcendentals=0
        ),
    )(place, tokens[0], tokens[1], tokens[2][1], tokens[3], gain, weight, *others)


def attention_kernel(place, lengths, query, m0, m1, m2, m3, wk, wv, wo, *refs):
    outs, columns = refs[:4], refs[4]
    x = place[2]
    blocks = (m0, m1, m2, m3)
    mine = pl.ds(pl.multiple_of(x * 512, 512), 512)
    for k, block in enumerate(blocks):
        columns[pl.ds(pl.multiple_of(((x - k) & 3) * 32, 32), 32), :] = block[:, mine]
    memory = jnp.concatenate([block[...] for block in blocks], 0)
    keys, values = (
        jnp.dot(memory, w[...], preferred_element_type=f32).astype(bf16) for w in (wk, wv)
    )
    spots = lax.broadcasted_iota(jnp.int32, (128, 128), 1)
    positions = (((x - (spots >> 5)) & 3) << 5) + (spots & 31)
    valid = positions < lengths[place[1]]
    contexts = []
    for h in range(2):
        at = slice(h * HEAD_DIM, (h + 1) * HEAD_DIM)
        scores = lax.dot_general(
            query[:, at], keys[:, at], (((1,), (1,)), ((), ())), preferred_element_type=f32
        )
        scores = jnp.where(valid, scores, -1e30)
        weights = jnp.exp(scores - jnp.max(scores, axis=-1, keepdims=True))
        probs = (weights / jnp.sum(weights, axis=-1, keepdims=True)).astype(bf16)
        contexts.append(jnp.dot(probs, values[:, at], preferred_element_type=f32).astype(bf16))
    context = jnp.concatenate(contexts, axis=1)
    for k in range(4):
        at = pl.ds(pl.multiple_of(((x + k) & 3) * 512, 512), 512)
        part = jnp.dot(context, wo[:, at], preferred_element_type=f32)
        outs[k][...] = part.astype(bf16)


def attention(place, lengths, query, memory, wk, wv, wo):
    return pl.pallas_call(
        attention_kernel,
        in_specs=[smem()] * 2 + [vmem()] * 8,
        out_specs=[vmem()] * 5,
        out_shape=[jax.ShapeDtypeStruct((128, 512), bf16)] * 5,
        compiler_params=params(16),
        cost_estimate=pl.CostEstimate(
            flops=6 * 128 * 2048 * 512, bytes_accessed=8 * MIB, transcendentals=128 * 256
        ),
    )(place, lengths, query, *memory, wk, wv, wo)


def shards(
    streams,
    lengths,
    encoder_gain,
    ffn_gate,
    ffn_lift,
    ffn_down,
    final_gain,
    decoder_gain,
    query_weight,
    key_weight,
    value_weight,
    output_weight,
):
    place = jnp.stack([lax.axis_index(a) for a in ("yh", "p", "x", "z", "c")]).astype(jnp.int32)
    p, x = place[1], place[2]
    local = streams[0].reshape(256, 512)

    def quarter(yh, p):
        start = (p * 2 + yh) * 512
        return jnp.concatenate(
            [lax.dynamic_slice_in_dim(w, start, 512, 1) for w in (ffn_gate, ffn_lift, ffn_down.T)]
        )

    own, rest = quarter(place[0], p), opposite(quarter(1 - place[0], 1 - p))
    near, far = jnp.concatenate([own, twin(own)]), jnp.concatenate([rest, twin(rest)])

    swapped = moved(local, ("p",), lambda a: (1 - a,))
    mine = jnp.where(p == 0, local, swapped)
    across = moved(local, ("yh", "p"), lambda a, b: (1 - a, 0) if b == 0 else None)
    corner = moved(local, ("yh", "p"), lambda a, b: (1 - a, 1) if b == 0 else None)
    theirs = jnp.where(p == 0, across, corner)
    decoding = jnp.where(p == 0, swapped[:128], local[128:])
    gain_rows = jnp.broadcast_to(final_gain[None], (16, 512))
    tokens = around(jnp.concatenate([mine, theirs, decoding, gain_rows]), 256)
    gain = encoder_gain.reshape(4, 1, 512)
    query_gain = decoder_gain.reshape(4, 1, 512)
    early = swapped, across, corner
    chunks = gather_lines(near, far, (early, (place, gain, query_gain), tokens[1:4:2]))

    terms = ffn(place, tokens, gain, chunks)
    terms = lax.all_to_all(terms, ("yh", "p", "x"), 0, 0)
    query, *others = query_rows(
        place, tokens, query_gain, query_weight, (key_weight, value_weight, output_weight)
    )
    memory = memory_rows(place, terms, tokens)
    memory = [shifted(memory, k) for k in range(4)]
    *attended, columns = attention(place, lengths, query, memory, *others)
    summed = decoding.astype(f32)
    for k in range(4):
        summed = summed + shifted(attended[k], k).astype(f32)
    decoded = summed.astype(bf16)
    swapped = moved(jnp.where(p == 0, decoded, columns), ("p",), lambda a: (1 - a,))
    first = jnp.where(p == 0, columns, swapped)
    second = jnp.where(p == 0, swapped, decoded)
    return jnp.concatenate([first, second]).reshape(1, 2, 128, 512)


def solution(mesh):
    names = tuple(SIZES)
    fine = Mesh(mesh.devices.reshape(tuple(SIZES.values())), names)
    dp = ("yh", "z", "c")
    placed = (
        P("p", dp, None, "x"),
        P(dp),
        P(),
        P(dp, "x"),
        P(dp, "x"),
        P("x", dp),
        P("x"),
        P(),
        P(None, "x"),
        P(None, "x"),
        P(None, "x"),
        P("x", None),
    )
    return jax.shard_map(
        shards, mesh=fine, in_specs=placed, out_specs=P("p", dp, None, "x"), check_vma=False
    )
```

```python
import jax
import jax.numpy as jnp
import numpy as np
from jax import lax
from jax.experimental import pallas as pl
from jax.experimental.pallas import tpu as pltpu
from jax.sharding import Mesh, PartitionSpec as P

HEAD_DIM = 256
epsilon = 1e-06
SIZES = {"yh": 2, "z": 8, "c": 2, "p": 2, "x": 4}
PLANE = ("yh", "p", "x")
bf16, f32 = jnp.bfloat16, jnp.float32
MIB = 1 << 20


def moved(value, axes, route):
    dims = [SIZES[a] for a in axes]
    pairs = []
    for at in np.ndindex(*dims):
        to = route(*at)
        if to is not None:
            pairs.append((int(np.ravel_multi_index(at, dims)), int(np.ravel_multi_index(to, dims))))
    return lax.ppermute(value, axes, pairs)


def passed(value):
    return moved(
        value, ("z", "c"), lambda z, c: ((z + 1) % 8, c) if c == 0 else ((z - 1) % 8, c)
    )


def after(value, *others):
    if not others:
        return value

    def kernel(*refs):
        del refs

    return pl.pallas_call(
        kernel,
        in_specs=[anyplace()] * (1 + len(others)),
        out_specs=anyplace(),
        out_shape=jax.ShapeDtypeStruct(value.shape, value.dtype),
        input_output_aliases={0: 0},
        compiler_params=params(1),
    )(value, *others)


def gather_lines(near, far, ready):
    near, far = [near], [far]
    for k in range(3):
        near.append(after(passed(near[k]), *ready[k]))
        far.append(passed(far[k]))
    near.append(passed(near[3][:192]))
    far.append(passed(far[3][:192]))
    return [v for line in (near, far) for v in line + [twin(chunk) for chunk in line[1:4]]]


def opposite(value):
    return moved(value, ("yh", "p"), lambda a, b: (1 - a, 1 - b))


def shifted(value, k):
    return moved(value, ("x",), lambda a: ((a + k) % 4,)) if k else value


def around(value, cut):
    up, down = (lambda a: ((a + 1) % 4,)), (lambda a: ((a - 1) % 4,))
    first, third = moved(value, ("x",), up), moved(value, ("x",), down)
    second = moved(first[:cut], ("x",), up), moved(third[cut:], ("x",), down)
    return value, first, second, third


def twin(value):
    return moved(value, ("c",), lambda a: (1 - a,))


def whole(shape):
    return pl.BlockSpec(shape, lambda *_: (0,) * len(shape))


def params(mib=60):
    return pltpu.CompilerParams(vmem_limit_bytes=mib * MIB)


def smem():
    return pl.BlockSpec(memory_space=pltpu.SMEM)


def vmem():
    return pl.BlockSpec(memory_space=pltpu.VMEM)


def anyplace():
    return pl.BlockSpec(memory_space=pl.ANY)


CHUNKS = 9


def normed_block(block, scale, gain):
    return (block[...].astype(f32) * scale * gain.astype(f32)).astype(bf16)


def scale_of(blocks):
    square = 0.0
    for block in blocks:
        t = block[...].astype(f32)
        square = square + jnp.sum(t * t, axis=-1, keepdims=True)
    return lax.rsqrt(square * (1.0 / 2048) + epsilon)


def halves_of(chunk, core, part):
    return [
        chunk[pl.ds(pl.multiple_of((a ^ core) * 192 + part * 64, 64), 64), :] for a in range(2)
    ]


def whole_chunks(place, chunks):
    yh, z, c = place[0], place[3], place[4]
    found = []
    for side in range(2):
        for k in (0, 1, 2, 3, 5, 6, 7):
            step, core = (k, c) if k < 5 else (k - 4, 1 - c)
            at = (yh ^ side) * 8 + ((z - step * (1 - 2 * core)) & 7)
            found.append((at, chunks[side * CHUNKS + k], core))
    return found


def first_kernel(place, *refs):
    tokens, gain, given = refs[:8], refs[8], refs[9:23]
    gate, lift, last, normed = refs[23:]
    yh, x, z = place[0], place[2], place[3]
    for i in range(2):
        rows = slice(i * 256, (i + 1) * 256)
        blocks = tokens[i * 4 : (i + 1) * 4]
        scale = scale_of(blocks)
        for k, block in enumerate(blocks):
            b = (x - k) & 3
            value = normed_block(block, scale, gain[b])
            for j in range(4):
                normed[b * 4 + j, rows] = value[:, j * 128 : (j + 1) * 128]
    chunks = [None] * (2 * CHUNKS)
    for j, chunk in enumerate(given):
        chunks[j // 7 * CHUNKS + (0, 1, 2, 3, 5, 6, 7)[j % 7]] = chunk
    spots = whole_chunks(place, chunks)
    for part, out in enumerate((gate, lift)):
        w = jnp.concatenate(
            [half for _, chunk, core in spots for half in halves_of(chunk, core, part)], 0
        )
        for i in range(2):
            rows = slice(i * 256, (i + 1) * 256)
            n = jnp.concatenate([normed[at, rows] for at, _, _ in spots], 1)
            out[rows] = jnp.dot(n, w, preferred_element_type=f32)
    for side in range(2):
        last[side] = normed[(yh ^ side) * 8 + ((z + 4) & 7)]


def second_kernel(place, gate, lift, last, *refs):
    chunks, out = refs[: 2 * CHUNKS], refs[2 * CHUNKS]
    yh, z, c = place[0], place[3], place[4]

    def rest_of(part):
        rows = slice(part * 64, (part + 1) * 64)
        found = []
        for side in range(2):
            own, twin = (chunks[side * CHUNKS + k][rows] for k in (4, 8))
            found += [jnp.where(c == 0, own, twin), jnp.where(c == 0, twin, own)]
        return jnp.concatenate(found, 0)

    n = jnp.concatenate([last[0], last[1]], 1)
    g = gate[...] + jnp.dot(n, rest_of(0), preferred_element_type=f32)
    up = lift[...] + jnp.dot(n, rest_of(1), preferred_element_type=f32)
    inner = 0.7978845608028654 * (g + 0.044715 * (g * g * g))
    hidden = (0.5 * g * (1.0 + jnp.tanh(inner)) * up).astype(bf16)
    spots = whole_chunks(place, chunks)
    pairs = [
        (
            [spots[k][0], spots[k + 1][0]],
            jnp.concatenate(halves_of(*spots[k][1:], 2) + halves_of(*spots[k + 1][1:], 2), 0),
        )
        for k in range(0, 14, 2)
    ]
    pairs.append(([(yh ^ side) * 8 + ((z + 4) & 7) for side in range(2)], rest_of(2)))
    for places, w in pairs:
        sums = lax.dot_general(hidden, w, (((1,), (1,)), ((), ())), preferred_element_type=f32)
        sums = sums.astype(bf16)
        for j, at in enumerate(places):
            lanes = pl.ds(pl.multiple_of((at & 3) * 128, 128), 128)
            out[:, at >> 2, :, lanes] = sums[:, j * 128 : (j + 1) * 128].reshape(8, 32, 128)


def rows_at(rows, at):
    return pl.BlockSpec((rows, 512), lambda i, place: (at, 0))


def ffn(place, tokens, gain, chunks):
    first, second, (third, third_rest), fourth = tokens
    mine, theirs = (first, second, third, fourth), (first, second, third_rest, fourth)
    given = [chunk for chunk in chunks if chunk.shape[0] == 384]
    grid_spec = pltpu.PrefetchScalarGridSpec(
        num_scalar_prefetch=1,
        grid=(1,),
        in_specs=[rows_at(256, at) for at in (0, 0, 0, 0, 1, 1, 0, 1)]
        + [whole(gain.shape)]
        + [vmem()] * len(given),
        out_specs=[vmem()] * 3,
        scratch_shapes=[pltpu.VMEM((16, 512, 128), bf16)],
    )
    gate, lift, last = pl.pallas_call(
        first_kernel,
        grid_spec=grid_spec,
        out_shape=[jax.ShapeDtypeStruct((512, 512), f32)] * 2
        + [jax.ShapeDtypeStruct((2, 512, 128), bf16)],
        compiler_params=params(24),
        cost_estimate=pl.CostEstimate(
            flops=512 * 1792 * 512 * 4, bytes_accessed=4 * MIB, transcendentals=0
        ),
    )(place, *mine, *theirs, gain, *given)
    lines = []
    for line in (chunks[: CHUNKS - 1], chunks[CHUNKS - 1 :]):
        arrived = after(line[4], last)
        lines += line[:4] + [arrived] + line[5:] + [twin(arrived)]
    chunks = lines
    grid_spec = pltpu.PrefetchScalarGridSpec(
        num_scalar_prefetch=1,
        grid=(2,),
        in_specs=[pl.BlockSpec((256, 512), lambda i, place: (i, 0))] * 2
        + [pl.BlockSpec((2, 256, 128), lambda i, place: (0, i, 0))]
        + [vmem()] * len(chunks),
        out_specs=pl.BlockSpec((8, 4, 32, 512), lambda i, place: (place[0] ^ i, 0, 0, 0)),
    )
    return pl.pallas_call(
        second_kernel,
        grid_spec=grid_spec,
        out_shape=jax.ShapeDtypeStruct((16, 4, 32, 512), bf16),
        compiler_params=params(24),
        cost_estimate=pl.CostEstimate(
            flops=512 * 2304 * 512 * 2, bytes_accessed=4 * MIB, transcendentals=512 * 512
        ),
    )(place, gate, lift, last, *chunks)


def memory_kernel(place, terms, *refs):
    tokens, gains, out = refs[:4], refs[4:8], refs[8]
    square, kept = 0.0, []
    for i in range(4):
        b = (place[2] - i) & 3
        total = terms[0, b].astype(f32)
        for k in range(1, 16):
            total = total + terms[k, b].astype(f32)
        merged = tokens[i][...].astype(f32) + total
        square = square + jnp.sum(merged * merged, axis=-1, keepdims=True)
        kept.append(merged)
    scale = lax.rsqrt(square * (1.0 / 2048) + epsilon)
    for i in range(4):
        at = pl.ds(pl.multiple_of(((place[2] - i) & 3) * 512, 512), 512)
        rounded = (kept[i] * scale * gains[i][:1].astype(f32)).astype(bf16)
        out[:, at] = rounded


def memory_rows(place, terms, tokens):
    first, second, (third, third_rest), fourth = tokens
    grid_spec = pltpu.PrefetchScalarGridSpec(
        num_scalar_prefetch=1,
        grid=(1,),
        in_specs=[whole(terms.shape)]
        + [pl.BlockSpec((32, 512), lambda i, place: (place[1] * 4 + place[2], 0))] * 4
        + [rows_at(16, at) for at in (40, 40, 24, 40)],
        out_specs=whole((32, 2048)),
    )
    return pl.pallas_call(
        memory_kernel,
        grid_spec=grid_spec,
        out_shape=jax.ShapeDtypeStruct((32, 2048), bf16),
        compiler_params=params(16),
    )(place, terms, first, second, third, fourth, first, second, third_rest, fourth)


def query_kernel(place, t0, t1, t2, t3, gain, weight, wk, wv, wo, out, *held):
    kept, sems = held[:3], held[3]
    copies = [
        pltpu.make_async_copy(source, target, sems.at[i])
        for i, (source, target) in enumerate(zip((wk, wv, wo), kept))
    ]
    for copy in copies:
        copy.start()
    blocks = (t0, t1, t2, t3)
    scale = scale_of(blocks)
    total = 0.0
    for k, block in enumerate(blocks):
        b = (place[2] - k) & 3
        rows = weight[pl.ds(pl.multiple_of(b * 512, 512), 512), :]
        n = normed_block(block, scale, gain[b])
        total += jnp.dot(n, rows, preferred_element_type=f32)
    out[...] = total.astype(bf16)
    for copy in copies:
        copy.wait()


def query_rows(place, tokens, gain, weight, others):
    grid_spec = pltpu.PrefetchScalarGridSpec(
        num_scalar_prefetch=1,
        grid=(1,),
        in_specs=[rows_at(128, at) for at in (4, 4, 2, 4)]
        + [whole(gain.shape), whole(weight.shape)]
        + [anyplace()] * 3,
        out_specs=[whole((128, 512))] + [vmem()] * 3,
        scratch_shapes=[pltpu.SemaphoreType.DMA((3,))],
    )
    return pl.pallas_call(
        query_kernel,
        grid_spec=grid_spec,
        out_shape=[jax.ShapeDtypeStruct((128, 512), bf16)]
        + [jax.ShapeDtypeStruct(w.shape, bf16) for w in others],
        compiler_params=params(40),
        cost_estimate=pl.CostEstimate(
            flops=2 * 128 * 2048 * 512, bytes_accessed=10 * MIB, transcendentals=0
        ),
    )(place, tokens[0], tokens[1], tokens[2][1], tokens[3], gain, weight, *others)


def attention_kernel(place, lengths, query, m0, m1, m2, m3, wk, wv, wo, *refs):
    outs, columns = refs[:4], refs[4]
    x = place[2]
    blocks = (m0, m1, m2, m3)
    mine = pl.ds(pl.multiple_of(x * 512, 512), 512)
    for k, block in enumerate(blocks):
        columns[pl.ds(pl.multiple_of(((x - k) & 3) * 32, 32), 32), :] = block[:, mine]
    memory = jnp.concatenate([block[...] for block in blocks], 0)
    keys, values = (
        jnp.dot(memory, w[...], preferred_element_type=f32).astype(bf16) for w in (wk, wv)
    )
    spots = lax.broadcasted_iota(jnp.int32, (128, 128), 1)
    positions = (((x - (spots >> 5)) & 3) << 5) + (spots & 31)
    valid = positions < lengths[place[1]]
    contexts = []
    for h in range(2):
        at = slice(h * HEAD_DIM, (h + 1) * HEAD_DIM)
        scores = lax.dot_general(
            query[:, at], keys[:, at], (((1,), (1,)), ((), ())), preferred_element_type=f32
        )
        scores = jnp.where(valid, scores, -1e30)
        weights = jnp.exp(scores - jnp.max(scores, axis=-1, keepdims=True))
        probs = (weights / jnp.sum(weights, axis=-1, keepdims=True)).astype(bf16)
        contexts.append(jnp.dot(probs, values[:, at], preferred_element_type=f32).astype(bf16))
    context = jnp.concatenate(contexts, axis=1)
    for k in range(4):
        at = pl.ds(pl.multiple_of(((x + k) & 3) * 512, 512), 512)
        part = jnp.dot(context, wo[:, at], preferred_element_type=f32)
        outs[k][...] = part.astype(bf16)


def attention(place, lengths, query, memory, wk, wv, wo):
    return pl.pallas_call(
        attention_kernel,
        in_specs=[smem()] * 2 + [vmem()] * 8,
        out_specs=[vmem()] * 5,
        out_shape=[jax.ShapeDtypeStruct((128, 512), bf16)] * 5,
        compiler_params=params(16),
        cost_estimate=pl.CostEstimate(
            flops=6 * 128 * 2048 * 512, bytes_accessed=8 * MIB, transcendentals=128 * 256
        ),
    )(place, lengths, query, *memory, wk, wv, wo)


def shards(
    streams,
    lengths,
    encoder_gain,
    ffn_gate,
    ffn_lift,
    ffn_down,
    final_gain,
    decoder_gain,
    query_weight,
    key_weight,
    value_weight,
    output_weight,
):
    place = jnp.stack([lax.axis_index(a) for a in ("yh", "p", "x", "z", "c")]).astype(jnp.int32)
    p, x = place[1], place[2]
    local = streams[0].reshape(256, 512)

    def quarter(yh, p):
        start = (p * 2 + yh) * 512
        return jnp.concatenate(
            [lax.dynamic_slice_in_dim(w, start, 512, 1) for w in (ffn_gate, ffn_lift, ffn_down.T)]
        )

    own, rest = quarter(place[0], p), opposite(quarter(1 - place[0], 1 - p))
    near, far = jnp.concatenate([own, twin(own)]), jnp.concatenate([rest, twin(rest)])

    swapped = moved(local, ("p",), lambda a: (1 - a,))
    mine = jnp.where(p == 0, local, swapped)
    across = moved(local, ("yh", "p"), lambda a, b: (1 - a, 0) if b == 0 else None)
    corner = moved(local, ("yh", "p"), lambda a, b: (1 - a, 1) if b == 0 else None)
    theirs = after(jnp.where(p == 0, across, corner), far)
    decoding = jnp.where(p == 0, swapped[:128], local[128:])
    gain_rows = jnp.broadcast_to(final_gain[None], (16, 512))
    tokens = around(jnp.concatenate([mine, theirs, decoding, gain_rows]), 256)
    gain = encoder_gain.reshape(4, 1, 512)
    query_gain = decoder_gain.reshape(4, 1, 512)
    early = swapped, across, corner
    chunks = gather_lines(near, far, (early, (place, gain, query_gain), tokens[1:4:2]))

    terms = ffn(place, tokens, gain, chunks)
    terms = lax.all_to_all(terms, ("yh", "p", "x"), 0, 0)
    query, *others = query_rows(
        place, tokens, query_gain, query_weight, (key_weight, value_weight, output_weight)
    )
    memory = memory_rows(place, terms, tokens)
    memory = [shifted(memory, k) for k in range(4)]
    *attended, columns = attention(place, lengths, query, memory, *others)
    summed = decoding.astype(f32)
    for k in range(4):
        summed = summed + shifted(attended[k], k).astype(f32)
    decoded = summed.astype(bf16)
    swapped = moved(jnp.where(p == 0, decoded, columns), ("p",), lambda a: (1 - a,))
    first = jnp.where(p == 0, columns, swapped)
    second = jnp.where(p == 0, swapped, decoded)
    return jnp.concatenate([first, second]).reshape(1, 2, 128, 512)


def solution(mesh):
    names = tuple(SIZES)
    fine = Mesh(mesh.devices.reshape(tuple(SIZES.values())), names)
    dp = ("yh", "z", "c")
    placed = (
        P("p", dp, None, "x"),
        P(dp),
        P(),
        P(dp, "x"),
        P(dp, "x"),
        P("x", dp),
        P("x"),
        P(),
        P(None, "x"),
        P(None, "x"),
        P(None, "x"),
        P("x", None),
    )
    return jax.shard_map(
        shards, mesh=fine, in_specs=placed, out_specs=P("p", dp, None, "x"), check_vma=False
    )
```
